256 devices in a mesh: leaf: 64 (over z, x, core), row: 4 (over y).
Axes of the slice: x: 4, y: 4, z: 8, core: 2. Of those that a mesh axis runs over, the one named last changes fastest.
Arguments:
- leaf_fronts: float32 [128, 8192, 512], P('leaf', 'row'), may hold values from -6 to 6
- front_rows: int32 [128], P('leaf'), may hold values from 768 to 8192, as said below
- parent_of: int32 [128], replicated, may hold values from 0 to 63, as said below
- column_map: int32 [128, 256], replicated, may hold values from 0 to 511, as said below
- parent_rows: float32 [64, 1024, 512], P('leaf', 'row'), may hold values from -6 to 6
Outputs:
- leaf_factor: float32 [128, 256, 512], P('leaf', None, 'row')
- parent_factor: float32 [64, 512, 512], P('leaf', None, 'row')
The draws below stay inside these ranges and needn't reach their ends.
Inputs may be any that keep to these rules, and one draw needn't show every extreme that they name: `front_rows`: each leaf front has at least 1.5 times as many live rows as columns; some front has all 8192 live and some exactly the fewest. `parent_of`: the parent of leaf front c is within 2 of c // 2, and some front's parent is exactly 2 away. `column_map`: the 256 entries of a row are distinct.
All inputs are finite; a program needn't handle non-finite values.
Results may differ from the reference program's by a relative error of at most 0.0003.
Values sent between devices are 32-bit elements; how exact they have to be, the bound alone decides.
A program may use at most 64 MiB of HBM per device.

```python
import jax
import jax.numpy as jnp
from jax import lax

W = 256
CB = 256
PF = 512
KIDS_DEV = 2
REACH = 2
F = 512
FRONTS = 128
PARENTS = 64
ROWS_ALL = 8192
PROWS_ALL = 1024


def draw_front_rows(key, part):
    key = jax.random.fold_in(key, 11)
    fewest = F + F // 2
    counts = jax.random.randint(key, (FRONTS,), fewest, ROWS_ALL + 1)
    counts = counts.at[0].set(ROWS_ALL).at[1].set(fewest)
    return counts.astype(jnp.int32)


def draw_parent_of(key, part):
    key = jax.random.fold_in(key, 12)
    devices_total = FRONTS // KIDS_DEV
    home_device = jnp.arange(FRONTS, dtype=jnp.int32) // KIDS_DEV
    offset = jax.random.randint(key, (FRONTS,), -REACH, REACH + 1)
    target = home_device + offset
    outside = (target < 0) | (target >= devices_total)
    target = jnp.where(outside, home_device - offset, target)
    target = target.at[0].set(REACH).at[1].set(0).at[FRONTS - 1].set(devices_total - 1)
    return target.astype(jnp.int32)


def draw_column_map(key, part):
    key = jax.random.fold_in(key, 13)
    row_keys = jax.random.split(key, FRONTS + 2)
    shuffled = jax.vmap(lambda row_key: jax.random.permutation(row_key, PF)[:CB])(row_keys[:FRONTS])
    upper_part = PF - CB + jax.random.permutation(row_keys[FRONTS], CB)
    lower_part = jax.random.permutation(row_keys[FRONTS + 1], CB)
    shuffled = shuffled.at[0].set(upper_part).at[1].set(lower_part)
    return shuffled.astype(jnp.int32)


def block_scale(rng, shape, cuts, low, top_value):
    def one(position, blocks):
        heights = jax.random.uniform(jax.random.fold_in(jax.random.fold_in(rng, 6), position), (blocks,), jnp.float32, low / len(cuts), top_value / len(cuts))
        return jnp.repeat(jnp.exp(heights), shape[position] // blocks).reshape((-1,) + (1,) * (len(shape) - position - 1))

    loudness = one(*cuts[0])
    for cut in cuts[1:]:
        loudness = loudness * one(*cut)
    return loudness


def noise(own_key, shape, scale, reach, cuts=(), kind=jnp.bfloat16):
    entries = scale * jax.random.normal(own_key, shape, jnp.float32)
    if cuts:
        entries = entries * block_scale(own_key, shape, cuts, -0.22, 0.18)
    return jnp.clip(entries, -reach, reach).astype(kind)


def setup_inputs(seed: int = 0) -> dict:
    key_list = jax.random.split(jax.random.key(seed), 6)
    return {
        "leaf_fronts": noise(key_list[0], (FRONTS, ROWS_ALL, F), 1.0, 6.0, ((0, 64), (1, 4)), jnp.float32),
        "front_rows": draw_front_rows(jax.random.fold_in(key_list[5], 71), 0),
        "parent_of": draw_parent_of(jax.random.fold_in(key_list[5], 71), 0),
        "column_map": draw_column_map(jax.random.fold_in(key_list[5], 71), 0),
        "parent_rows": noise(key_list[4], (PARENTS, PROWS_ALL, PF), 1.0, 6.0, ((0, 64), (1, 4)), jnp.float32),
    }


HIGHEST = lax.Precision.HIGHEST

def front_gram(front_block):
    return jnp.dot(front_block.T, front_block, precision=HIGHEST)

def reference(leaf_fronts, front_rows, parent_of, column_map, parent_rows):
    positions = jnp.arange(ROWS_ALL, dtype=jnp.int32)

    def factor_leaf(inputs):
        front_block, length = inputs
        masked = jnp.where(positions[:, None] < length, front_block, 0.0)
        gram_matrix = front_gram(masked) / ROWS_ALL
        return jnp.linalg.cholesky(gram_matrix).T
    uppers = lax.map(factor_leaf, (leaf_fronts, front_rows))
    leaf_factor = uppers[:, :W, :]
    contribution = uppers[:, W:, W:]
    own_grams = lax.map(lambda parent_block: front_gram(parent_block) / PROWS_ALL, parent_rows)

    def add_child(parent_grams, inputs):
        contribution_rows, parent, mapping = inputs
        child_gram = jnp.dot(contribution_rows.T, contribution_rows, precision=HIGHEST)
        parent_grams = parent_grams.at[parent, mapping[:, None], mapping[None, :]].add(child_gram)
        return (parent_grams, None)
    parent_grams, unused = lax.scan(add_child, own_grams, (contribution, parent_of, column_map))
    parent_factor = lax.map(lambda matrix: jnp.linalg.cholesky(matrix).T, parent_grams)
    return (leaf_factor, parent_factor)
```

```python
import jax
import jax.numpy as jnp
from jax import lax
from jax.experimental import pallas as pl
from jax.experimental.pallas import tpu as pltpu
from jax.sharding import PartitionSpec as P

F32, BF16 = jnp.float32, jnp.bfloat16
MESH = pl.DeviceIdType.MESH
N = 512
H = 128
BLOCKS = [(i, j) for i in range(4) for j in range(i, 4)]
CHUNKS = ((0, 1), (1, 4), (4, 7), (7, 10))
REACH = 2


def split(x):
    high = x.astype(BF16)
    return high, (x - high.astype(F32)).astype(BF16)


def nn(a, b):
    return jnp.dot(a, b, preferred_element_type=F32)


def tn(a, b):
    return lax.dot_general(a, b, (((0,), (0,)), ((), ())), preferred_element_type=F32)


def nt(a, b):
    return lax.dot_general(a, b, (((1,), (1,)), ((), ())), preferred_element_type=F32)


def nn3(a, b):
    ah, al = split(a)
    bh, bl = split(b)
    return nn(ah, bh) + (nn(ah, bl) + nn(al, bh))


def spread_row(x, p):
    return jnp.broadcast_to(x[p : p + 1, :], (8, H))


def spread_column(x, k):
    return jnp.broadcast_to(x[:, k : k + 1], (8, H))


def tree(terms):
    while len(terms) > 1:
        terms = [terms[i] + terms[i + 1] for i in range(0, len(terms), 2)]
    return terms[0]


def factor_block(a):
    sub = lax.broadcasted_iota(jnp.int32, (8, H), 0)
    lane = lax.broadcasted_iota(jnp.int32, (8, H), 1)
    count = H // 8
    tiles = [[a[8 * t : 8 * t + 8, :], (lane == sub + 8 * t).astype(F32)] for t in range(count)]
    factor, inverse = [], []
    for t in range(count):
        j = 8 * t
        left, right = tiles[t]
        column = [spread_column(left, j + k) for k in range(8)]
        if t + 1 < count:
            following = [spread_column(tiles[t + 1][0], j + k) for k in range(8)]
        frow = jnp.zeros((8, H), F32)
        irow = jnp.zeros((8, H), F32)
        for p in range(8):
            here = sub == p
            pivot = spread_row(column[p], p)
            inv = 1.0 / pivot
            root = lax.rsqrt(pivot)

            def eliminate(z):
                row = spread_row(z, p)
                return jnp.where(here, row * inv, z - (column[p] * row) * inv)

            frow = jnp.where(here, left * root, frow)
            irow = jnp.where(here, right * root, irow)
            for k in range(p + 1, 8):
                column[k] = eliminate(column[k])
            left, right = eliminate(left), eliminate(right)
        factor.append(jnp.where(lane >= sub + j, frow, 0.0))
        inverse.append(irow)
        if t + 1 < count:
            nxt = [
                old - tree([following[p] * spread_row(new, p) for p in range(8)])
                for old, new in zip(tiles[t + 1], (left, right))
            ]
            if t + 2 < count:
                below = jnp.concatenate([tiles[u][0] for u in range(t + 2, count)], 0)
                parts = [jnp.concatenate([left, right], 1)]
                if j:
                    parts = [jnp.zeros((j, 2 * H), F32)] + parts
                parts.append(jnp.zeros((H - 8 - j, 2 * H), F32))
                change = nn3(below, jnp.concatenate(parts, 0))
                for u in range(t + 2, count):
                    rows = change[8 * (u - t - 2) : 8 * (u - t - 1)]
                    tiles[u] = [tiles[u][0] - rows[:, :H], tiles[u][1] - rows[:, H:]]
            tiles[t + 1] = nxt
    return jnp.concatenate(factor, 0), jnp.concatenate(inverse, 0)


def kernel(
    rows_ref, parent_ref, map_ref, leaf_hbm, prow_hbm, lf_out, pf_out,
    xs, ps, hh, hl, gram, far, near, work, fac, fac_h, fac_l, rleaf, rpar, slots,
    load_sem, far_send, far_recv, near_send, near_recv, lf_send, lf_recv, slot_send, slot_recv, pf_send, pf_recv,
):
    r = lax.axis_index("row")
    l = lax.axis_index("leaf")
    leaves = lax.axis_size("leaf")
    core = lax.rem(l, 2)
    live_rows = xs.shape[1]
    pieces = load_sem.shape[1]
    piece = live_rows // pieces

    def mod4(v):
        return lax.rem(v + 8, 4)

    place = [mod4(r - (2 * core + k)) for k in range(2)]
    first = jnp.where(jnp.logical_or(place[0] == 0, place[0] == 3), 1, 0)
    rp = 3 - 2 * core
    place.append(mod4(r - rp))

    def load(step, c):
        k = first if step == 0 else 1 - first
        part = pl.ds(c * piece, piece)
        return pltpu.make_async_copy(leaf_hbm.at[k, part], xs.at[k, part], load_sem.at[step, c])

    for step in range(2):
        for c in range(pieces):
            load(step, c).start()
    prow_copy = pltpu.make_async_copy(prow_hbm.at[0], ps, load_sem.at[2, 0])
    prow_copy.start()

    barrier = pltpu.get_barrier_semaphore()
    for step in (1, 2, 3):
        pl.semaphore_signal(barrier, inc=1, device_id={"row": mod4(r + step)}, device_id_type=MESH)
    greeted = 3
    for delta in (-2, -1, 1, 2):
        inside = jnp.logical_and(l + delta >= 0, l + delta < leaves)

        @pl.when(inside)
        def _(delta=delta):
            pl.semaphore_signal(barrier, inc=1, device_id={"leaf": l + delta}, device_id_type=MESH)

        greeted = greeted + jnp.where(inside, 1, 0)
    pl.semaphore_wait(barrier, greeted)

    def far_copy(u, ci, side):
        b0, b1 = CHUNKS[ci]
        return pltpu.make_async_remote_copy(
            src_ref=gram.at[u, b0:b1, pl.ds(64 * side, 64)],
            dst_ref=far.at[u, b0:b1],
            send_sem=far_send.at[u, side, ci],
            recv_sem=far_recv.at[u, ci],
            device_id={"row": mod4(r - 1 + 2 * side)},
            device_id_type=MESH,
        )

    def near_copy(u, ci, side):
        b0, b1 = CHUNKS[ci]
        return pltpu.make_async_remote_copy(
            src_ref=gram.at[u, b0:b1],
            dst_ref=near.at[u, side, b0:b1],
            send_sem=near_send.at[u, ci],
            recv_sem=near_recv.at[u, side, ci],
            device_id={"row": mod4(r - 1 + 2 * side)},
            device_id_type=MESH,
        )

    def start_far(u):
        @pl.when(place[u] == 2)
        def _():
            for ci in range(len(CHUNKS)):
                for side in range(2):
                    far_copy(u, ci, side).start()

    def forward(u):
        for side in range(2):

            @pl.when(place[u] == 1 + 2 * side)
            def _(side=side):
                for ci, (b0, b1) in enumerate(CHUNKS):
                    far_copy(u, ci, side).wait_recv()
                    half = pl.ds(64 * side, 64)
                    gram[u, b0:b1, half] = gram[u, b0:b1, half] + far[u, b0:b1]
                    near_copy(u, ci, side).start()

    def wait_near(u, ci):
        for side in range(2):
            near_copy(u, ci, side).wait_recv()

    def drain(u):
        @pl.when(place[u] == 2)
        def _():
            for ci in range(len(CHUNKS)):
                for side in range(2):
                    far_copy(u, ci, side).wait_send()

        for side in range(2):

            @pl.when(place[u] == 1 + 2 * side)
            def _(side=side):
                for ci in range(len(CHUNKS)):
                    near_copy(u, ci, side).wait_send()

    def summed(u, b):
        return gram[u, b] + (near[u, 0, b] + near[u, 1, b])

    def add_gram(x, start):
        high, low = split(x)
        for ref, rows, columns, other in (
            (hh, slice(0, 256), slice(0, N), high),
            (hh, slice(256, N), slice(256, N), high),
            (hl, slice(0, N), slice(0, N), low),
        ):
            value = tn(high[:, rows], other[:, columns])
            ref[rows, columns] = value if start else ref[rows, columns] + value

    def finish_gram(u, scale):
        for b, (i, j) in enumerate(BLOCKS):
            rows, columns = slice(H * i, H * i + H), slice(H * j, H * j + H)
            gram[u, b] = (hh[rows, columns] + (hl[rows, columns] + hl[columns, rows].T)) * scale

    total = 4 * live_rows
    for step in range(2):
        k = first if step == 0 else 1 - first
        live = rows_ref[k] - r * live_rows
        for c in range(pieces):
            load(step, c).wait()
            x = xs[k, pl.ds(c * piece, piece)]
            position = lax.broadcasted_iota(jnp.int32, (piece, N), 0) + c * piece
            add_gram(jnp.where(position < live, x, 0.0), c == 0)
        finish_gram(k, 1.0 / total)
        if step == 0:
            start_far(0)
            start_far(1)
    forward(0)
    forward(1)
    prow_copy.wait()
    add_gram(ps[...], True)
    finish_gram(2, 1.0 / (4 * ps.shape[0]))

    block_of = lax.broadcasted_iota(jnp.int32, (H, N), 1) // H

    def factor_rows(b, out):
        columns = pl.ds(pl.multiple_of(b * H, H), H)

        @pl.when(b > 0)
        def _():
            high, low = fac_h[:, columns], fac_l[:, columns]
            whole_h, whole_l = fac_h[...], fac_l[...]
            work[b] = work[b] - (tn(high, whole_h) + (tn(high, whole_l) + tn(low, whole_h)))

        diagonal, inverse = factor_block(work[b, :, columns])
        panel = jnp.where(block_of > b, nn3(inverse, work[b]), 0.0)
        fac[...] = panel
        fac[:, columns] = diagonal
        here = pl.ds(pl.multiple_of(b * H, H), H)
        fac_h[here], fac_l[here] = split(fac[...])
        for q in range(4):
            out[b, q] = fac[:, q * H : q * H + H]

    def fill_rows(u, ci):
        wait_near(u, ci)
        b0, b1 = CHUNKS[ci]
        for b in range(b0, b1):
            i, j = BLOCKS[b]
            work[i, :, j * H : j * H + H] = summed(u, b)

    k_mine = r - 2 * core
    factors = jnp.logical_and(k_mine >= 0, k_mine < 2)

    def lf_copy(k, b, q):
        return pltpu.make_async_remote_copy(
            src_ref=rleaf.at[b, q],
            dst_ref=lf_out.at[k, b * H : b * H + H],
            send_sem=lf_send.at[b, q],
            recv_sem=lf_recv.at[k, b],
            device_id={"row": q},
            device_id_type=MESH,
        )

    def slot_copy(delta):
        return pltpu.make_async_remote_copy(
            src_ref=slots.at[2],
            dst_ref=slots.at[2 + delta],
            send_sem=slot_send.at[2 + delta],
            recv_sem=slot_recv.at[2 + delta],
            device_id={"leaf": l + delta},
            device_id_type=MESH,
        )

    work[...] = jnp.zeros_like(work)
    fac_h[...] = jnp.zeros_like(fac_h)
    fac_l[...] = jnp.zeros_like(fac_l)

    @pl.when(factors)
    def _():
        def step(b, carry):
            @pl.when(b == 0)
            def _():
                for k in range(2):

                    @pl.when(k_mine == k)
                    def _(k=k):
                        fill_rows(k, 0)
                        fill_rows(k, 1)

            @pl.when(b == 1)
            def _():
                for k in range(2):

                    @pl.when(k_mine == k)
                    def _(k=k):
                        fill_rows(k, 2)

            factor_rows(b, rleaf)
            for q in range(4):

                @pl.when(jnp.logical_and(q != r, q >= b))
                def _(q=q):
                    for k in range(2):
                        for bb in range(2):

                            @pl.when(jnp.logical_and(k_mine == k, b == bb))
                            def _(k=k, bb=bb):
                                lf_copy(k, bb, q).start()

            return carry

        lax.fori_loop(0, 2, step, 0)
        for k in range(2):

            @pl.when(k_mine == k)
            def _(k=k):
                wait_near(k, 3)
                for b in range(2):

                    for q in range(4):

                        @pl.when(jnp.logical_and(q == r, q >= b))
                        def _(q=q, b=b):
                            lf_out[k, b * H : b * H + H] = rleaf[b, q]

        for i in range(2):
            rows = slice(256 + H * i, 384 + H * i)
            columns = slice(256 + H * i, N)
            left_h, left_l = fac_h[0:256, rows], fac_l[0:256, rows]
            right_h, right_l = fac_h[0:256, columns], fac_l[0:256, columns]
            taken = tn(left_h, right_h) + (tn(left_h, right_l) + tn(left_l, right_h))
            for j in range(i, 2):
                b = 7 + i + j
                slots[2, i + j] = summed(k_mine, b) - taken[:, (j - i) * H : (j - i) * H + H]
        for delta in (-2, -1, 1, 2):

            @pl.when(jnp.logical_and(l + delta >= 0, l + delta < leaves))
            def _(delta=delta):
                slot_copy(delta).start()

    for k in range(2):

        @pl.when(r == 0)
        def _(k=k):
            lf_out[k, H : 2 * H] = jnp.zeros((H, H), F32)

    for b in range(1, 4):

        @pl.when(b > r)
        def _(b=b):
            pf_out[0, b * H : b * H + H] = jnp.zeros((H, H), F32)

    even = lax.rem(l, 2) == r // 2

    for delta in range(-REACH, REACH + 1):
        source = l - delta
        parity = even if delta % 2 == 0 else jnp.logical_not(even)
        valid = jnp.logical_and(parity, jnp.logical_and(source >= 0, source < leaves))

        @pl.when(valid)
        def _(delta=delta, source=source):
            if delta != 0:
                slot_copy(delta).wait_recv()
            front = 2 * source + lax.rem(r, 2)
            away = jnp.where(parent_ref[front] == l, 0, 2 * N)
            target = map_ref[pl.ds(front, 1), :] + away
            chosen = (lax.broadcasted_iota(jnp.int32, (N, 256), 0) == target).astype(F32).astype(BF16)
            s = slots[2 + delta]
            square = jnp.concatenate(
                [jnp.concatenate([s[0], s[1]], 1), jnp.concatenate([s[1].T, s[2]], 1)], 0
            )
            high, low = split(square)
            high_rows, low_rows = nn(chosen, high).astype(BF16), nn(chosen, low).astype(BF16)
            for half in range(2):
                rows, columns = slice(256 * half, 256 * half + 256), slice(256 * half, N)
                placed = nt(high_rows[rows], chosen[columns]) + nt(low_rows[rows], chosen[columns])
                for b, (i, j) in enumerate(BLOCKS):
                    if i // 2 == half:
                        ii, jj = (i - 2 * half) * H, (j - 2 * half) * H
                        gram[2, b] = gram[2, b] + placed[ii : ii + H, jj : jj + H]

    start_far(2)
    forward(2)

    def pf_copy(b, q):
        return pltpu.make_async_remote_copy(
            src_ref=rpar.at[b, q],
            dst_ref=pf_out.at[0, b * H : b * H + H],
            send_sem=pf_send.at[b, q],
            recv_sem=pf_recv.at[b],
            device_id={"row": q},
            device_id_type=MESH,
        )

    @pl.when(place[2] == 0)
    def _():
        fac_h[...] = jnp.zeros_like(fac_h)
        fac_l[...] = jnp.zeros_like(fac_l)

        def step(b, carry):
            for ci in range(1, 4):

                @pl.when(b == ci - 1)
                def _(ci=ci):
                    if ci == 1:
                        fill_rows(2, 0)
                    fill_rows(2, ci)
            @pl.when(b == 2)
            def _():
                pass

            factor_rows(b, rpar)
            for q in range(4):
                for bb in range(q + 1):

                    @pl.when(jnp.logical_and(q != r, b == bb))
                    def _(q=q, bb=bb):
                        pf_copy(bb, q).start()

                    @pl.when(jnp.logical_and(q == r, b == bb))
                    def _(q=q, bb=bb):
                        pf_out[0, bb * H : bb * H + H] = rpar[bb, q]

            return carry

        lax.fori_loop(0, 4, step, 0)
        for q in range(4):

            @pl.when(q != r)
            def _(q=q):
                for bb in range(q + 1):
                    pf_copy(bb, q).wait_send()

    @pl.when(place[2] != 0)
    def _():
        for bb in range(4):

            @pl.when(bb <= r)
            def _(bb=bb):
                pf_copy(bb, 0).wait_recv()

    for k in range(2):

        @pl.when(k_mine != k)
        def _(k=k):
            lf_copy(k, 0, 0).wait_recv()

            @pl.when(r > 0)
            def _():
                lf_copy(k, 1, 0).wait_recv()

        @pl.when(k_mine == k)
        def _(k=k):
            for q in range(4):

                @pl.when(q != r)
                def _(q=q):
                    for b in range(min(q, 1) + 1):
                        lf_copy(k, b, q).wait_send()

    @pl.when(factors)
    def _():
        for delta in (-2, -1, 1, 2):

            @pl.when(jnp.logical_and(l + delta >= 0, l + delta < leaves))
            def _(delta=delta):
                slot_copy(delta).wait_send()

    for u in range(3):
        drain(u)


def per_device(leaf_fronts, front_rows, parent_of, column_map, parent_rows):
    kids, live_rows, _ = leaf_fronts.shape
    chunks = len(CHUNKS)
    dma = pltpu.SemaphoreType.DMA
    vmem = pltpu.VMEM
    return pl.pallas_call(
        kernel,
        out_shape=(
            jax.ShapeDtypeStruct((kids, 256, H), F32),
            jax.ShapeDtypeStruct((1, N, H), F32),
        ),
        in_specs=[
            pl.BlockSpec(memory_space=pltpu.SMEM),
            pl.BlockSpec(memory_space=pltpu.SMEM),
            pl.BlockSpec(memory_space=pltpu.VMEM),
            pl.BlockSpec(memory_space=pl.ANY),
            pl.BlockSpec(memory_space=pl.ANY),
        ],
        out_specs=(pl.BlockSpec(memory_space=pltpu.VMEM),) * 2,
        scratch_shapes=[
            vmem((kids, live_rows, N), F32),
            vmem(parent_rows.shape[1:], F32),
            vmem((N, N), F32),
            vmem((N, N), F32),
            vmem((3, 10, H, H), F32),
            vmem((3, 10, H // 2, H), F32),
            vmem((3, 2, 10, H, H), F32),
            vmem((4, H, N), F32),
            vmem((H, N), F32),
            vmem((N, N), BF16),
            vmem((N, N), BF16),
            vmem((2, 4, H, H), F32),
            vmem((4, 4, H, H), F32),
            vmem((5, 3, H, H), F32),
            dma((3, 2)),
            dma((3, 2, chunks)),
            dma((3, chunks)),
            dma((3, chunks)),
            dma((3, 2, chunks)),
            dma((2, 4)),
            dma((2, 2)),
            dma((5,)),
            dma((5,)),
            dma((4, 4)),
            dma((4,)),
        ],
        compiler_params=pltpu.CompilerParams(
            collective_id=0, has_side_effects=True, vmem_limit_bytes=48 << 20
        ),
        name="fronts",
    )(front_rows, parent_of, column_map, leaf_fronts, parent_rows)


def solution(mesh):
    return jax.shard_map(
        per_device,
        mesh=mesh,
        in_specs=(P("leaf", "row", None), P("leaf"), P(), P(), P("leaf", "row", None)),
        out_specs=(P("leaf", None, "row"), P("leaf", None, "row")),
        check_vma=False,
    )
```

```python
import jax
import jax.numpy as jnp
from jax import lax
from jax.experimental import pallas as pl
from jax.experimental.pallas import tpu as pltpu
from jax.sharding import PartitionSpec as P

F32, BF16 = jnp.float32, jnp.bfloat16
MESH = pl.DeviceIdType.MESH
N = 512
H = 128
BLOCKS = [(i, j) for i in range(4) for j in range(i, 4)]
CHUNKS = ((1, 4), (4, 7), (7, 10))
REACH = 2


def split(x):
    high = x.astype(BF16)
    return high, (x - high.astype(F32)).astype(BF16)


def nn(a, b):
    return jnp.dot(a, b, preferred_element_type=F32)


def tn(a, b):
    return lax.dot_general(a, b, (((0,), (0,)), ((), ())), preferred_element_type=F32)


def nt(a, b):
    return lax.dot_general(a, b, (((1,), (1,)), ((), ())), preferred_element_type=F32)


def nn3(a, b):
    ah, al = split(a)
    bh, bl = split(b)
    return nn(ah, bh) + (nn(ah, bl) + nn(al, bh))


def nn3_stacked(a, b):
    ah, al = split(a)
    bh, bl = split(b)
    return nn(jnp.concatenate([ah, al, ah], 1), jnp.concatenate([bh, bh, bl], 0))


def tn3(ah, al, bh, bl):
    return tn(ah, bh) + (tn(ah, bl) + tn(al, bh))


def spread_row(x, p):
    return jnp.broadcast_to(x[p : p + 1, :], (8, H))


def spread_column(x, k):
    return jnp.take_along_axis(x, jnp.full((8, H), k, jnp.int32), axis=1)


def tree(terms):
    while len(terms) > 1:
        terms = [terms[i] + terms[i + 1] for i in range(0, len(terms), 2)]
    return terms[0]


def factor_block(a):
    sub = lax.broadcasted_iota(jnp.int32, (8, H), 0)
    lane = lax.broadcasted_iota(jnp.int32, (8, H), 1)
    count = H // 8
    tiles = [[a[8 * t : 8 * t + 8, :], (lane == sub + 8 * t).astype(F32)] for t in range(count)]
    factor, inverse = [], []
    for t in range(count):
        j = 8 * t
        left, right = tiles[t]
        column = [spread_column(left, j + k) for k in range(8)]
        if t + 1 < count:
            following = [spread_column(tiles[t + 1][0], j + k) for k in range(8)]
        frow = jnp.zeros((8, H), F32)
        irow = jnp.zeros((8, H), F32)
        for p in range(8):
            here = sub == p
            pivot = spread_row(column[p], p)
            inv = 1.0 / pivot
            root = lax.rsqrt(pivot)

            signed = jnp.where(here, -1.0, column[p])

            def eliminate(z):
                return jnp.where(here, 0.0, z) - (signed * spread_row(z, p)) * inv

            frow = jnp.where(here, left * root, frow)
            irow = jnp.where(here, right * root, irow)
            for k in range(p + 1, 8):
                column[k] = eliminate(column[k])
            left, right = eliminate(left), eliminate(right)
        factor.append(jnp.where(lane >= sub + j, frow, 0.0))
        inverse.append(irow)
        if t + 1 < count:
            nxt = [
                old - tree([following[p] * spread_row(new, p) for p in range(8)])
                for old, new in zip(tiles[t + 1], (left, right))
            ]
            if t + 2 < count:
                below = jnp.concatenate([tiles[u][0] for u in range(t + 2, count)], 0)
                parts = [jnp.concatenate([left, right], 1)]
                if j:
                    parts = [jnp.zeros((j, 2 * H), F32)] + parts
                parts.append(jnp.zeros((H - 8 - j, 2 * H), F32))
                change = nn3_stacked(below, jnp.concatenate(parts, 0))
                for u in range(t + 2, count):
                    rows = change[8 * (u - t - 2) : 8 * (u - t - 1)]
                    tiles[u] = [tiles[u][0] - rows[:, :H], tiles[u][1] - rows[:, H:]]
            tiles[t + 1] = nxt
    return jnp.concatenate(factor, 0), jnp.concatenate(inverse, 0)


def kernel(
    rows_hbm, parent_hbm, map_hbm, leaf_hbm, prow_hbm, lf_out, pf_out,
    rows_ref, parent_ref, map_ref, xs, ps, hh, hl, gram, far, near, direct,
    work, diag, upd, fac, fac_h, fac_l, rleaf, rpar, slots,
    load_sem, small_sem, direct_send, direct_recv, far_send, far_recv, near_send, near_recv,
    lf_send, lf_recv, slot_send, slot_recv, pf_send, pf_recv,
):
    r = lax.axis_index("row")
    l = lax.axis_index("leaf")
    leaves = lax.axis_size("leaf")
    core = lax.rem(l, 2)
    live_rows = xs.shape[1]
    pieces = load_sem.shape[1]
    piece = live_rows // pieces

    def mod4(v):
        return lax.rem(v + 8, 4)

    place = [mod4(r - (2 * core + k)) for k in range(2)]
    first = jnp.where(jnp.logical_or(place[0] == 0, place[0] == 3), 1, 0)
    rp = 3 - 2 * core
    place.append(mod4(r - rp))
    k_mine = r - 2 * core
    factors = jnp.logical_and(k_mine >= 0, k_mine < 2)
    k_here = jnp.clip(k_mine, 0, 1)

    barrier = pltpu.get_barrier_semaphore()
    for step in (1, 2, 3):
        pl.semaphore_signal(barrier, inc=1, device_id={"row": mod4(r + step)}, device_id_type=MESH)
    greeted = 3
    for delta in (-2, -1, 1, 2):
        inside = jnp.logical_and(l + delta >= 0, l + delta < leaves)

        @pl.when(inside)
        def _(delta=delta):
            pl.semaphore_signal(barrier, inc=1, device_id={"leaf": l + delta}, device_id_type=MESH)

        greeted = greeted + jnp.where(inside, 1, 0)

    def load(step, c):
        k = first if step == 0 else 1 - first
        part = pl.ds(c * piece, piece)
        return pltpu.make_async_copy(leaf_hbm.at[k, part], xs.at[k, part], load_sem.at[step, c])

    small = [
        pltpu.make_async_copy(rows_hbm, rows_ref, small_sem.at[0]),
        pltpu.make_async_copy(parent_hbm, parent_ref, small_sem.at[1]),
        pltpu.make_async_copy(map_hbm, map_ref, small_sem.at[2]),
        pltpu.make_async_copy(prow_hbm.at[0], ps, small_sem.at[3]),
    ]
    small[0].start()
    for step in range(2):
        for c in range(pieces):
            load(step, c).start()
    for copy in small[1:]:
        copy.start()

    def direct_copy(u):
        return pltpu.make_async_remote_copy(
            src_ref=gram.at[u, 0],
            dst_ref=direct.at[u],
            send_sem=direct_send.at[u],
            recv_sem=direct_recv.at[u],
            device_id={"row": mod4(r + 2)},
            device_id_type=MESH,
        )

    def far_copy(u, ci, side):
        b0, b1 = CHUNKS[ci]
        return pltpu.make_async_remote_copy(
            src_ref=gram.at[u, b0:b1, pl.ds(64 * side, 64)],
            dst_ref=far.at[u, b0:b1],
            send_sem=far_send.at[u, side, ci],
            recv_sem=far_recv.at[u, ci],
            device_id={"row": mod4(r - 1 + 2 * side)},
            device_id_type=MESH,
        )

    def near_copy(u, ci, side):
        b0, b1 = CHUNKS[ci] if ci >= 0 else (0, 1)
        return pltpu.make_async_remote_copy(
            src_ref=gram.at[u, b0:b1],
            dst_ref=near.at[u, side, b0:b1],
            send_sem=near_send.at[u, ci + 1],
            recv_sem=near_recv.at[u, side, ci + 1],
            device_id={"row": mod4(r - 1 + 2 * side)},
            device_id_type=MESH,
        )

    def start_first(u):
        @pl.when(place[u] == 2)
        def _():
            direct_copy(u).start()
            for ci in range(len(CHUNKS)):
                for side in range(2):
                    far_copy(u, ci, side).start()

        for side in range(2):

            @pl.when(place[u] == 1 + 2 * side)
            def _(side=side):
                near_copy(u, -1, side).start()

    def forward(u):
        for side in range(2):

            @pl.when(place[u] == 1 + 2 * side)
            def _(side=side):
                for ci, (b0, b1) in enumerate(CHUNKS):
                    far_copy(u, ci, side).wait_recv()
                    half = pl.ds(64 * side, 64)
                    gram[u, b0:b1, half] = gram[u, b0:b1, half] + far[u, b0:b1]
                    near_copy(u, ci, side).start()

    def wait_near(u, ci):
        if ci < 0:
            direct_copy(u).wait_recv()
        for side in range(2):
            near_copy(u, ci, side).wait_recv()

    def drain(u):
        @pl.when(place[u] == 2)
        def _():
            direct_copy(u).wait_send()
            for ci in range(len(CHUNKS)):
                for side in range(2):
                    far_copy(u, ci, side).wait_send()

        for side in range(2):

            @pl.when(place[u] == 1 + 2 * side)
            def _(side=side):
                for ci in range(-1, len(CHUNKS)):
                    near_copy(u, ci, side).wait_send()

    def summed(u, b):
        return gram[u, b] + (near[u, 0, b] + near[u, 1, b])

    def add_gram(x, start):
        high, low = split(x)
        for ref, rows, columns, other in (
            (hh, slice(0, 256), slice(0, N), high),
            (hh, slice(256, N), slice(256, N), high),
            (hl, slice(0, N), slice(0, N), low),
        ):
            value = tn(high[:, rows], other[:, columns])
            ref[rows, columns] = value if start else ref[rows, columns] + value

    def finish_gram(u, scale):
        for b, (i, j) in enumerate(BLOCKS):
            rows, columns = slice(H * i, H * i + H), slice(H * j, H * j + H)
            gram[u, b] = (hh[rows, columns] + (hl[rows, columns] + hl[columns, rows].T)) * scale

    total = 4 * live_rows
    small[0].wait()
    for step in range(2):
        k = first if step == 0 else 1 - first
        live = rows_ref[k] - r * live_rows
        for c in range(pieces):
            load(step, c).wait()
            x = xs[k, pl.ds(c * piece, piece)]
            position = lax.broadcasted_iota(jnp.int32, (piece, N), 0) + c * piece
            add_gram(jnp.where(position < live, x, 0.0), c == 0)
        finish_gram(k, 1.0 / total)
        if step == 0:
            pl.semaphore_wait(barrier, greeted)
        for u in range(2):

            @pl.when(k == u)
            def _(u=u):
                start_first(u)

    forward(0)
    forward(1)

    block_of = lax.broadcasted_iota(jnp.int32, (H, N), 1) // H

    def fill_rows(u, ci):
        wait_near(u, ci)
        b0, b1 = CHUNKS[ci]
        for b in range(b0, b1):
            i, j = BLOCKS[b]
            work[i, :, j * H : j * H + H] = summed(u, b)

    def factor_rows(u, b, out):
        columns = pl.ds(pl.multiple_of(b * H, H), H)
        later = jnp.minimum(b + 1, 3)
        ncolumns = pl.ds(pl.multiple_of(later * H, H), H)
        whole_h, whole_l = fac_h[...], fac_l[...]
        upd[:, 0:N] = tn3(fac_h[:, columns], fac_l[:, columns], whole_h, whole_l)
        nh, nl = fac_h[:, ncolumns], fac_l[:, ncolumns]
        upd[:, N : N + H] = tn3(nh, nl, nh, nl)
        diagonal, inverse = factor_block(diag[...])

        @pl.when(b == 0)
        def _():
            fill_rows(u, 0)
            fill_rows(u, 1)

        @pl.when(b == 1)
        def _():
            fill_rows(u, 2)

        panel = jnp.where(block_of > b, nn3(inverse, work[b] - upd[:, 0:N]), 0.0)
        fac[...] = panel
        fac[:, columns] = diagonal
        here = pl.ds(pl.multiple_of(b * H, H), H)
        fac_h[here], fac_l[here] = split(fac[...])
        nh, nl = split(fac[:, ncolumns])
        diag[...] = (work[later, :, ncolumns] - upd[:, N : N + H]) - tn3(nh, nl, nh, nl)
        for q in range(4):
            out[b, q] = fac[:, q * H : q * H + H]

    def lf_copy(k, b, q):
        return pltpu.make_async_remote_copy(
            src_ref=rleaf.at[b, q],
            dst_ref=lf_out.at[k, pl.ds(b * H, H)],
            send_sem=lf_send.at[b, q],
            recv_sem=lf_recv.at[k, b],
            device_id={"row": q},
            device_id_type=MESH,
        )

    def slot_copy(delta):
        return pltpu.make_async_remote_copy(
            src_ref=slots.at[2],
            dst_ref=slots.at[2 + delta],
            send_sem=slot_send.at[2 + delta],
            recv_sem=slot_recv.at[2 + delta],
            device_id={"leaf": l + delta},
            device_id_type=MESH,
        )

    @pl.when(factors)
    def _():
        fac_h[...] = jnp.zeros_like(fac_h)
        fac_l[...] = jnp.zeros_like(fac_l)
        wait_near(k_here, -1)
        diag[...] = summed(k_here, 0) + direct[k_here]

        def step(b, carry):
            factor_rows(k_here, b, rleaf)
            return carry

        lax.fori_loop(0, 2, step, 0)
        slots[2, 0] = diag[...]
        rows = slice(384, N)
        columns = slice(256, N)
        taken = tn3(
            fac_h[0:256, rows], fac_l[0:256, rows], fac_h[0:256, columns], fac_l[0:256, columns]
        )
        slots[2, 1] = work[2, :, 384:N] - taken[:, 0:H].T
        slots[2, 2] = work[3, :, 384:N] - taken[:, H : 2 * H]
        for delta in (-2, -1, 1, 2):

            @pl.when(jnp.logical_and(l + delta >= 0, l + delta < leaves))
            def _(delta=delta):
                slot_copy(delta).start()

        for q in range(4):
            for b in range(min(q, 1) + 1):

                @pl.when(q != r)
                def _(q=q, b=b):
                    lf_copy(k_here, b, q).start()

                @pl.when(q == r)
                def _(q=q, b=b):
                    lf_out[k_here, b * H : b * H + H] = rleaf[b, q]

    for copy in small[1:]:
        copy.wait()
    add_gram(ps[...], True)
    finish_gram(2, 1.0 / (4 * ps.shape[0]))
    for k in range(2):

        @pl.when(r == 0)
        def _(k=k):
            lf_out[k, H : 2 * H] = jnp.zeros((H, H), F32)

    for b in range(1, 4):

        @pl.when(b > r)
        def _(b=b):
            pf_out[0, b * H : b * H + H] = jnp.zeros((H, H), F32)

    @pl.when(place[2] == 0)
    def _():
        fac_h[...] = jnp.zeros_like(fac_h)
        fac_l[...] = jnp.zeros_like(fac_l)

    even = lax.rem(l, 2) == r // 2

    for delta in (0, 1, -1, 2, -2):
        source = l - delta
        parity = even if delta % 2 == 0 else jnp.logical_not(even)
        valid = jnp.logical_and(parity, jnp.logical_and(source >= 0, source < leaves))

        @pl.when(valid)
        def _(delta=delta, source=source):
            if delta != 0:
                slot_copy(delta).wait_recv()
            front = 2 * source + lax.rem(r, 2)
            away = jnp.where(parent_ref[front] == l, 0, 2 * N)
            target = map_ref[pl.ds(front, 1), :] + away
            chosen = (lax.broadcasted_iota(jnp.int32, (N, 256), 0) == target).astype(F32).astype(BF16)
            s = slots[2 + delta]
            square = jnp.concatenate(
                [jnp.concatenate([s[0], s[1]], 1), jnp.concatenate([s[1].T, s[2]], 1)], 0
            )
            high, low = split(square)
            high_rows, low_rows = nn(chosen, high).astype(BF16), nn(chosen, low).astype(BF16)
            for half in range(2):
                rows, columns = slice(256 * half, 256 * half + 256), slice(256 * half, N)
                placed = nt(high_rows[rows], chosen[columns]) + nt(low_rows[rows], chosen[columns])
                for b, (i, j) in enumerate(BLOCKS):
                    if i // 2 == half:
                        ii, jj = (i - 2 * half) * H, (j - 2 * half) * H
                        gram[2, b] = gram[2, b] + placed[ii : ii + H, jj : jj + H]

    start_first(2)
    forward(2)

    def pf_copy(b, q):
        return pltpu.make_async_remote_copy(
            src_ref=rpar.at[b, q],
            dst_ref=pf_out.at[0, pl.ds(b * H, H)],
            send_sem=pf_send.at[b, q],
            recv_sem=pf_recv.at[b],
            device_id={"row": q},
            device_id_type=MESH,
        )

    @pl.when(place[2] == 0)
    def _():
        wait_near(2, -1)
        diag[...] = summed(2, 0) + direct[2]

        def step(b, carry):
            factor_rows(2, b, rpar)
            for q in range(4):

                @pl.when(jnp.logical_and(q != r, q >= b))
                def _(q=q):
                    pf_copy(b, q).start()

                @pl.when(jnp.logical_and(q == r, q >= b))
                def _(q=q):
                    pf_out[0, pl.ds(pl.multiple_of(b * H, H), H)] = rpar[b, q]

            return carry

        lax.fori_loop(0, 4, step, 0)
        for q in range(4):

            @pl.when(q != r)
            def _(q=q):
                for b in range(q + 1):
                    pf_copy(b, q).wait_send()

    @pl.when(place[2] != 0)
    def _():
        for b in range(4):

            @pl.when(b <= r)
            def _(b=b):
                pf_copy(b, 0).wait_recv()

    for k in range(2):

        @pl.when(k_mine != k)
        def _(k=k):
            lf_copy(k, 0, 0).wait_recv()

            @pl.when(r > 0)
            def _():
                lf_copy(k, 1, 0).wait_recv()

        @pl.when(k_mine == k)
        def _(k=k):
            for q in range(4):

                @pl.when(q != r)
                def _(q=q):
                    for b in range(min(q, 1) + 1):
                        lf_copy(k, b, q).wait_send()

    @pl.when(factors)
    def _():
        for delta in (-2, -1, 1, 2):

            @pl.when(jnp.logical_and(l + delta >= 0, l + delta < leaves))
            def _(delta=delta):
                slot_copy(delta).wait_send()

    for u in range(3):
        drain(u)


def per_device(leaf_fronts, front_rows, parent_of, column_map, parent_rows):
    kids, live_rows, _ = leaf_fronts.shape
    chunks = len(CHUNKS)
    dma = pltpu.SemaphoreType.DMA
    vmem = pltpu.VMEM
    return pl.pallas_call(
        kernel,
        out_shape=(
            jax.ShapeDtypeStruct((kids, 256, H), F32),
            jax.ShapeDtypeStruct((1, N, H), F32),
        ),
        in_specs=[pl.BlockSpec(memory_space=pl.ANY)] * 5,
        out_specs=(pl.BlockSpec(memory_space=pltpu.VMEM),) * 2,
        scratch_shapes=[
            pltpu.SMEM(front_rows.shape, jnp.int32),
            pltpu.SMEM(parent_of.shape, jnp.int32),
            vmem(column_map.shape, jnp.int32),
            vmem((kids, live_rows, N), F32),
            vmem(parent_rows.shape[1:], F32),
            vmem((N, N), F32),
            vmem((N, N), F32),
            vmem((3, 10, H, H), F32),
            vmem((3, 10, H // 2, H), F32),
            vmem((3, 2, 10, H, H), F32),
            vmem((3, H, H), F32),
            vmem((4, H, N), F32),
            vmem((H, H), F32),
            vmem((H, N + H), F32),
            vmem((H, N), F32),
            vmem((N, N), BF16),
            vmem((N, N), BF16),
            vmem((2, 4, H, H), F32),
            vmem((4, 4, H, H), F32),
            vmem((5, 3, H, H), F32),
            dma((2, 2)),
            dma((4,)),
            dma((3,)),
            dma((3,)),
            dma((3, 2, chunks)),
            dma((3, chunks)),
            dma((3, chunks + 1)),
            dma((3, 2, chunks + 1)),
            dma((2, 4)),
            dma((2, 2)),
            dma((5,)),
            dma((5,)),
            dma((4, 4)),
            dma((4,)),
        ],
        compiler_params=pltpu.CompilerParams(
            collective_id=0, has_side_effects=True, vmem_limit_bytes=60 << 20
        ),
        name="fronts",
    )(front_rows, parent_of, column_map, leaf_fronts, parent_rows)


def solution(mesh):
    return jax.shard_map(
        per_device,
        mesh=mesh,
        in_specs=(P("leaf", "row", None), P("leaf"), P(), P(), P("leaf", "row", None)),
        out_specs=(P("leaf", None, "row"), P("leaf", None, "row")),
        check_vma=False,
    )
```

```python
import jax
import jax.numpy as jnp
from jax import lax
from jax.experimental import pallas as pl
from jax.experimental.pallas import tpu as pltpu
from jax.sharding import PartitionSpec as P

F32, BF16 = jnp.float32, jnp.bfloat16
MESH = pl.DeviceIdType.MESH
N = 512
H = 128
BLOCKS = [(i, j) for i in range(4) for j in range(i, 4)]
CHUNKS = ((1, 4), (4, 7), (7, 10))
REACH = 2


def split(x):
    high = x.astype(BF16)
    return high, (x - high.astype(F32)).astype(BF16)


def nn(a, b):
    return jnp.dot(a, b, preferred_element_type=F32)


def tn(a, b):
    return lax.dot_general(a, b, (((0,), (0,)), ((), ())), preferred_element_type=F32)


def nt(a, b):
    return lax.dot_general(a, b, (((1,), (1,)), ((), ())), preferred_element_type=F32)


def nn3(a, b):
    ah, al = split(a)
    bh, bl = split(b)
    return nn(ah, bh) + (nn(ah, bl) + nn(al, bh))


def nn3_stacked(a, b):
    ah, al = split(a)
    bh, bl = split(b)
    return nn(jnp.concatenate([ah, al, ah], 1), jnp.concatenate([bh, bh, bl], 0))


def tn3(ah, al, bh, bl):
    return tn(ah, bh) + (tn(ah, bl) + tn(al, bh))


def spread_row(x, p):
    return jnp.broadcast_to(x[p : p + 1, :], (8, H))


def spread_column(x, k):
    return jnp.take_along_axis(x, jnp.full((8, H), k, jnp.int32), axis=1)


def tree(terms):
    while len(terms) > 1:
        terms = [terms[i] + terms[i + 1] for i in range(0, len(terms), 2)]
    return terms[0]


def factor_block(a):
    sub = lax.broadcasted_iota(jnp.int32, (8, H), 0)
    lane = lax.broadcasted_iota(jnp.int32, (8, H), 1)
    count = H // 8
    tiles = [[a[8 * t : 8 * t + 8, :], (lane == sub + 8 * t).astype(F32)] for t in range(count)]
    factor, inverse = [], []
    for t in range(count):
        j = 8 * t
        left, right = tiles[t]
        column = [spread_column(left, j + k) for k in range(8)]
        if t + 1 < count:
            following = [spread_column(tiles[t + 1][0], j + k) for k in range(8)]
        frow = jnp.zeros((8, H), F32)
        irow = jnp.zeros((8, H), F32)
        for p in range(8):
            here = sub == p
            pivot = spread_row(column[p], p)
            inv = 1.0 / pivot
            root = lax.rsqrt(pivot)

            signed = jnp.where(here, -1.0, column[p])

            def eliminate(z):
                return jnp.where(here, 0.0, z) - (signed * spread_row(z, p)) * inv

            frow = jnp.where(here, left * root, frow)
            irow = jnp.where(here, right * root, irow)
            for k in range(p + 1, 8):
                column[k] = eliminate(column[k])
            left, right = eliminate(left), eliminate(right)
        factor.append(jnp.where(lane >= sub + j, frow, 0.0))
        inverse.append(irow)
        if t + 1 < count:
            nxt = [
                old - tree([following[p] * spread_row(new, p) for p in range(8)])
                for old, new in zip(tiles[t + 1], (left, right))
            ]
            if t + 2 < count:
                below = jnp.concatenate([tiles[u][0] for u in range(t + 2, count)], 0)
                parts = [jnp.concatenate([left, right], 1)]
                if j:
                    parts = [jnp.zeros((j, 2 * H), F32)] + parts
                parts.append(jnp.zeros((H - 8 - j, 2 * H), F32))
                change = nn3_stacked(below, jnp.concatenate(parts, 0))
                for u in range(t + 2, count):
                    rows = change[8 * (u - t - 2) : 8 * (u - t - 1)]
                    tiles[u] = [tiles[u][0] - rows[:, :H], tiles[u][1] - rows[:, H:]]
            tiles[t + 1] = nxt
    return jnp.concatenate(factor, 0), jnp.concatenate(inverse, 0)


def kernel(
    rows_hbm, parent_hbm, map_hbm, leaf_hbm, prow_hbm, lf_out, pf_out,
    rows_ref, parent_ref, map_ref, xs, ps, hh, hl, gram, far, near, direct,
    work, diag, rleaf, rpar, slots,
    load_sem, small_sem, direct_send, direct_recv, far_send, far_recv, near_send, near_recv,
    lf_send, lf_recv, slot_send, slot_recv, pf_send, pf_recv,
):
    r = lax.axis_index("row")
    l = lax.axis_index("leaf")
    leaves = lax.axis_size("leaf")
    core = lax.rem(l, 2)
    live_rows = xs.shape[1]
    pieces = load_sem.shape[1]
    piece = live_rows // pieces

    def mod4(v):
        return lax.rem(v + 8, 4)

    place = [mod4(r - (2 * core + k)) for k in range(2)]
    first = jnp.where(jnp.logical_or(place[0] == 0, place[0] == 3), 1, 0)
    rp = 3 - 2 * core
    place.append(mod4(r - rp))
    k_mine = r - 2 * core
    factors = jnp.logical_and(k_mine >= 0, k_mine < 2)
    k_here = jnp.clip(k_mine, 0, 1)

    barrier = pltpu.get_barrier_semaphore()
    for step in (1, 2, 3):
        pl.semaphore_signal(barrier, inc=1, device_id={"row": mod4(r + step)}, device_id_type=MESH)
    greeted = 3
    for delta in (-2, -1, 1, 2):
        there = jnp.logical_and(l + delta >= 0, l + delta < leaves)

        @pl.when(there)
        def _(delta=delta):
            pl.semaphore_signal(barrier, inc=1, device_id={"leaf": l + delta}, device_id_type=MESH)

        greeted = greeted + jnp.where(there, 1, 0)

    def load(step, c):
        k = first if step == 0 else 1 - first
        part = pl.ds(c * piece, piece)
        return pltpu.make_async_copy(leaf_hbm.at[k, part], xs.at[k, part], load_sem.at[step, c])

    small = [
        pltpu.make_async_copy(rows_hbm, rows_ref, small_sem.at[0]),
        pltpu.make_async_copy(parent_hbm, parent_ref, small_sem.at[1]),
        pltpu.make_async_copy(map_hbm, map_ref, small_sem.at[2]),
        pltpu.make_async_copy(prow_hbm.at[0], ps, small_sem.at[3]),
    ]
    small[0].start()
    for step in range(2):
        for c in range(pieces):
            load(step, c).start()
    for copy in small[1:]:
        copy.start()

    def direct_copy(u):
        return pltpu.make_async_remote_copy(
            src_ref=gram.at[u, 0],
            dst_ref=direct.at[u],
            send_sem=direct_send.at[u],
            recv_sem=direct_recv.at[u],
            device_id={"row": mod4(r + 2)},
            device_id_type=MESH,
        )

    def far_copy(u, ci, side):
        b0, b1 = CHUNKS[ci]
        return pltpu.make_async_remote_copy(
            src_ref=gram.at[u, b0:b1, pl.ds(64 * side, 64)],
            dst_ref=far.at[u, b0:b1],
            send_sem=far_send.at[u, side, ci],
            recv_sem=far_recv.at[u, ci],
            device_id={"row": mod4(r - 1 + 2 * side)},
            device_id_type=MESH,
        )

    def near_copy(u, ci, side):
        b0, b1 = CHUNKS[ci] if ci >= 0 else (0, 1)
        return pltpu.make_async_remote_copy(
            src_ref=gram.at[u, b0:b1],
            dst_ref=near.at[u, side, b0:b1],
            send_sem=near_send.at[u, ci + 1],
            recv_sem=near_recv.at[u, side, ci + 1],
            device_id={"row": mod4(r - 1 + 2 * side)},
            device_id_type=MESH,
        )

    def start_first(u):
        @pl.when(place[u] == 2)
        def _():
            direct_copy(u).start()
            for ci in range(len(CHUNKS)):
                for side in range(2):
                    far_copy(u, ci, side).start()

        for side in range(2):

            @pl.when(place[u] == 1 + 2 * side)
            def _(side=side):
                near_copy(u, -1, side).start()

    def forward(u, which):
        for side in range(2):

            @pl.when(place[u] == 1 + 2 * side)
            def _(side=side):
                for ci in which:
                    b0, b1 = CHUNKS[ci]
                    far_copy(u, ci, side).wait_recv()
                    half = pl.ds(64 * side, 64)
                    gram[u, b0:b1, half] = gram[u, b0:b1, half] + far[u, b0:b1]
                    near_copy(u, ci, side).start()

    def wait_near(u, ci):
        if ci < 0:
            direct_copy(u).wait_recv()
        for side in range(2):
            near_copy(u, ci, side).wait_recv()

    def drain(u):
        @pl.when(place[u] == 2)
        def _():
            direct_copy(u).wait_send()
            for ci in range(len(CHUNKS)):
                for side in range(2):
                    far_copy(u, ci, side).wait_send()

        for side in range(2):

            @pl.when(place[u] == 1 + 2 * side)
            def _(side=side):
                for ci in range(-1, len(CHUNKS)):
                    near_copy(u, ci, side).wait_send()

    def summed(u, b):
        return gram[u, b] + (near[u, 0, b] + near[u, 1, b])

    def add_gram(x, start):
        high, low = split(x)
        for ref, rows, columns, other in (
            (hh, slice(0, 256), slice(0, N), high),
            (hh, slice(256, N), slice(256, N), high),
            (hl, slice(0, N), slice(0, N), low),
        ):
            value = tn(high[:, rows], other[:, columns])
            ref[rows, columns] = value if start else ref[rows, columns] + value

    def finish_gram(u, scale):
        for b, (i, j) in enumerate(BLOCKS):
            rows, columns = slice(H * i, H * i + H), slice(H * j, H * j + H)
            gram[u, b] = (hh[rows, columns] + (hl[rows, columns] + hl[columns, rows].T)) * scale

    total = 4 * live_rows
    small[0].wait()
    for step in range(2):
        k = first if step == 0 else 1 - first
        live = rows_ref[k] - r * live_rows
        for c in range(pieces):
            load(step, c).wait()
            x = xs[k, pl.ds(c * piece, piece)]
            position = lax.broadcasted_iota(jnp.int32, (piece, N), 0) + c * piece
            add_gram(jnp.where(position < live, x, 0.0), c == 0)
        finish_gram(k, 1.0 / total)
        if step == 0:
            pl.semaphore_wait(barrier, greeted)
        for u in range(2):

            @pl.when(k == u)
            def _(u=u):
                start_first(u)

    for u in range(2):
        forward(u, (0, 1))

    def fill_rows(u, ci, add):
        wait_near(u, ci)
        b0, b1 = CHUNKS[ci]
        for b in range(b0, b1):
            i, j = BLOCKS[b]
            columns = slice(j * H, j * H + H)
            work[i, :, columns] = work[i, :, columns] + summed(u, b) if add else summed(u, b)

    def factor(u, count, out, beside, after):
        wait_near(u, -1)
        diag[...] = summed(u, 0) + direct[u]
        for b in range(count):
            diagonal, inverse = factor_block(diag[...])
            out[b, b] = diagonal
            beside(b)
            if b < 3:
                if b == 0:
                    fill_rows(u, 0, False)
                    fill_rows(u, 1, False)
                if b == 1:
                    fill_rows(u, 2, True)
                lo = b * H + H
                ih, il = split(inverse)

                def solve(columns):
                    wh, wl = split(work[b, :, columns])
                    return nn(ih, wh) + (nn(ih, wl) + nn(il, wh))

                near_panel = solve(slice(lo, lo + H))
                nh, nl = split(near_panel)
                out[b, b + 1] = near_panel
                if b == 0:
                    diag[...] = work[1, :, lo : lo + H] - tn3(nh, nl, nh, nl)
                else:
                    diag[...] = work[b + 1, :, lo : lo + H] - tn3(nh, nl, nh, nl)
                if b < 2:
                    rest = solve(slice(lo + H, N))
                    rh, rl = split(rest)
                    for q in range(b + 2, 4):
                        out[b, q] = rest[:, (q - b - 2) * H : (q - b - 1) * H]
                    columns = slice(lo + H, N)
                    work[b + 1, :, columns] = work[b + 1, :, columns] - tn3(nh, nl, rh, rl)
                    for i in range(b + 2, 4):
                        o = (i - b - 2) * H
                        columns = slice(i * H, N)
                        taken = tn3(rh[:, o : o + H], rl[:, o : o + H], rh[:, o:], rl[:, o:])
                        work[i, :, columns] = -taken if b == 0 else work[i, :, columns] - taken
            after(b)

    def lf_copy(k, b, q):
        return pltpu.make_async_remote_copy(
            src_ref=rleaf.at[b, q],
            dst_ref=lf_out.at[k, pl.ds(b * H, H)],
            send_sem=lf_send.at[b, q],
            recv_sem=lf_recv.at[k, b],
            device_id={"row": q},
            device_id_type=MESH,
        )

    def slot_copy(delta):
        return pltpu.make_async_remote_copy(
            src_ref=slots.at[2],
            dst_ref=slots.at[2 + delta],
            send_sem=slot_send.at[2 + delta],
            recv_sem=slot_recv.at[2 + delta],
            device_id={"leaf": l + delta},
            device_id_type=MESH,
        )

    sibling = l + 1 - 2 * core
    onward = 4 * core - 2

    def slot_copy(source, slot, device, send):
        return pltpu.make_async_remote_copy(
            src_ref=slots.at[source],
            dst_ref=slots.at[slot],
            send_sem=slot_send.at[send],
            recv_sem=slot_recv.at[slot],
            device_id={"leaf": device},
            device_id_type=MESH,
        )

    def inside(place_of):
        return jnp.logical_and(place_of >= 0, place_of < leaves)

    def own_slot(delta):
        return slot_copy(2, 2 + delta, l + delta, 2 + delta)

    def sibling_slot():
        return slot_copy(2, 2 + sibling - l, sibling, 1)

    def onward_slot():
        return slot_copy(2 + onward, 1 + 2 * core, sibling, 2)

    @pl.when(factors)
    def _():
        def beside(b):
            if b == 0:
                for u in range(2):
                    forward(u, (2,))

        factor(k_here, 2, rleaf, beside, lambda b: None)
        slots[2, 0] = diag[...]
        slots[2, 1] = work[2, :, 384:N]
        slots[2, 2] = work[3, :, 384:N]
        for delta in (-2, 2):

            @pl.when(inside(l + delta))
            def _(delta=delta):
                own_slot(delta).start()

        sibling_slot().start()
        for q in range(4):
            for b in range(min(q, 1) + 1):

                @pl.when(q != r)
                def _(q=q, b=b):
                    lf_copy(k_here, b, q).start()

                @pl.when(q == r)
                def _(q=q, b=b):
                    lf_out[k_here, b * H : b * H + H] = rleaf[b, q]

    @pl.when(jnp.logical_not(factors))
    def _():
        for u in range(2):
            forward(u, (2,))

    for copy in small[1:]:
        copy.wait()
    add_gram(ps[...], True)
    finish_gram(2, 1.0 / (4 * ps.shape[0]))
    for k in range(2):

        @pl.when(r == 0)
        def _(k=k):
            lf_out[k, H : 2 * H] = jnp.zeros((H, H), F32)

    for b in range(1, 4):

        @pl.when(b > r)
        def _(b=b):
            pf_out[0, b * H : b * H + H] = jnp.zeros((H, H), F32)

    def place_slot(i, carry):
        one = 2 * core - 1
        delta = jnp.where(
            factors,
            jnp.where(i == 0, 0, jnp.where(i == 1, onward, -onward)),
            jnp.where(i == 0, one, -one),
        )
        source = l - delta
        valid = jnp.logical_and(jnp.logical_or(factors, i < 2), inside(source))

        @pl.when(valid)
        def _():
            slot = 2 + delta

            @pl.when(delta != 0)
            def _():
                slot_copy(2, slot, sibling, 0).wait_recv()

            @pl.when(jnp.logical_and(factors, i == 1))
            def _():
                onward_slot().start()

            front = 2 * source + lax.rem(r, 2)
            away = jnp.where(parent_ref[front] == l, 0, 2 * N)
            target = map_ref[pl.ds(front, 1), :] + away
            chosen = (lax.broadcasted_iota(jnp.int32, (N, 256), 0) == target).astype(F32).astype(BF16)
            s = slots[slot]
            square = jnp.concatenate(
                [jnp.concatenate([s[0], s[1]], 1), jnp.concatenate([s[1].T, s[2]], 1)], 0
            )
            high, low = split(square)
            high_rows, low_rows = nn(chosen, high).astype(BF16), nn(chosen, low).astype(BF16)
            for half in range(2):
                rows, columns = slice(256 * half, 256 * half + 256), slice(256 * half, N)
                placed = nt(high_rows[rows], chosen[columns]) + nt(low_rows[rows], chosen[columns])
                for b, (bi, bj) in enumerate(BLOCKS):
                    if bi // 2 == half:
                        ii, jj = (bi - 2 * half) * H, (bj - 2 * half) * H
                        gram[2, b] = gram[2, b] + placed[ii : ii + H, jj : jj + H]

        return carry

    lax.fori_loop(0, 3, place_slot, 0)

    start_first(2)
    forward(2, (0, 1, 2))

    def pf_copy(b, q):
        return pltpu.make_async_remote_copy(
            src_ref=rpar.at[b, q],
            dst_ref=pf_out.at[0, pl.ds(b * H, H)],
            send_sem=pf_send.at[b, q],
            recv_sem=pf_recv.at[b],
            device_id={"row": q},
            device_id_type=MESH,
        )

    @pl.when(place[2] == 0)
    def _():
        def after(b):
            for q in range(b, 4):

                @pl.when(q != r)
                def _(q=q):
                    pf_copy(b, q).start()

                @pl.when(q == r)
                def _(q=q):
                    pf_out[0, b * H : b * H + H] = rpar[b, q]

        factor(2, 4, rpar, lambda b: None, after)
        for q in range(4):

            @pl.when(q != r)
            def _(q=q):
                for b in range(q + 1):
                    pf_copy(b, q).wait_send()

    @pl.when(place[2] != 0)
    def _():
        for b in range(4):

            @pl.when(b <= r)
            def _(b=b):
                pf_copy(b, 0).wait_recv()

    for k in range(2):

        @pl.when(k_mine != k)
        def _(k=k):
            lf_copy(k, 0, 0).wait_recv()

            @pl.when(r > 0)
            def _():
                lf_copy(k, 1, 0).wait_recv()

        @pl.when(k_mine == k)
        def _(k=k):
            for q in range(4):

                @pl.when(q != r)
                def _(q=q):
                    for b in range(min(q, 1) + 1):
                        lf_copy(k, b, q).wait_send()

    @pl.when(factors)
    def _():
        for delta in (-2, 2):

            @pl.when(inside(l + delta))
            def _(delta=delta):
                own_slot(delta).wait_send()

        sibling_slot().wait_send()

        @pl.when(inside(l - onward))
        def _():
            onward_slot().wait_send()

    for u in range(3):
        drain(u)


def per_device(leaf_fronts, front_rows, parent_of, column_map, parent_rows):
    kids, live_rows, _ = leaf_fronts.shape
    chunks = len(CHUNKS)
    dma = pltpu.SemaphoreType.DMA
    vmem = pltpu.VMEM
    return pl.pallas_call(
        kernel,
        out_shape=(
            jax.ShapeDtypeStruct((kids, 256, H), F32),
            jax.ShapeDtypeStruct((1, N, H), F32),
        ),
        in_specs=[pl.BlockSpec(memory_space=pltpu.HBM)] * 5,
        out_specs=(pl.BlockSpec(memory_space=pltpu.VMEM),) * 2,
        scratch_shapes=[
            pltpu.SMEM(front_rows.shape, jnp.int32),
            pltpu.SMEM(parent_of.shape, jnp.int32),
            vmem(column_map.shape, jnp.int32),
            vmem((kids, live_rows, N), F32),
            vmem(parent_rows.shape[1:], F32),
            vmem((N, N), F32),
            vmem((N, N), F32),
            vmem((3, 10, H, H), F32),
            vmem((3, 10, H // 2, H), F32),
            vmem((3, 2, 10, H, H), F32),
            vmem((3, H, H), F32),
            vmem((4, H, N), F32),
            vmem((H, H), F32),
            vmem((2, 4, H, H), F32),
            vmem((4, 4, H, H), F32),
            vmem((5, 3, H, H), F32),
            dma((2, 2)),
            dma((4,)),
            dma((3,)),
            dma((3,)),
            dma((3, 2, chunks)),
            dma((3, chunks)),
            dma((3, chunks + 1)),
            dma((3, 2, chunks + 1)),
            dma((2, 4)),
            dma((2, 2)),
            dma((5,)),
            dma((5,)),
            dma((4, 4)),
            dma((4,)),
        ],
        compiler_params=pltpu.CompilerParams(
            collective_id=0, has_side_effects=True, vmem_limit_bytes=60 << 20
        ),
        name="fronts",
    )(front_rows, parent_of, column_map, leaf_fronts, parent_rows)


def solution(mesh):
    return jax.shard_map(
        per_device,
        mesh=mesh,
        in_specs=(P("leaf", "row", None), P("leaf"), P(), P(), P("leaf", "row", None)),
        out_specs=(P("leaf", None, "row"), P("leaf", None, "row")),
        check_vma=False,
    )
```

```python
import jax
import jax.numpy as jnp
from jax import lax
from jax.experimental import pallas as pl
from jax.experimental.pallas import tpu as pltpu
from jax.sharding import PartitionSpec as P

F32, BF16 = jnp.float32, jnp.bfloat16
MESH = pl.DeviceIdType.MESH
N = 512
H = 128
BLOCKS = [(i, j) for i in range(4) for j in range(i, 4)]
CHUNKS = ((1, 4), (4, 7), (7, 10))
REACH = 2


def split(x):
    high = x.astype(BF16)
    return high, (x - high.astype(F32)).astype(BF16)


def nn(a, b):
    return jnp.dot(a, b, preferred_element_type=F32)


def tn(a, b):
    return lax.dot_general(a, b, (((0,), (0,)), ((), ())), preferred_element_type=F32)


def nt(a, b):
    return lax.dot_general(a, b, (((1,), (1,)), ((), ())), preferred_element_type=F32)


def nn3(a, b):
    ah, al = split(a)
    bh, bl = split(b)
    return nn(ah, bh) + (nn(ah, bl) + nn(al, bh))


def nn3_stacked(a, b):
    ah, al = split(a)
    bh, bl = split(b)
    return nn(jnp.concatenate([ah, al, ah], 1), jnp.concatenate([bh, bh, bl], 0))


def tn3(ah, al, bh, bl):
    return tn(ah, bh) + (tn(ah, bl) + tn(al, bh))


def spread_row(x, p):
    return jnp.broadcast_to(x[p : p + 1, :], (8, H))


def spread_column(x, k):
    return jnp.take_along_axis(x, jnp.full((8, H), k, jnp.int32), axis=1)


def tree(terms):
    while len(terms) > 1:
        terms = [terms[i] + terms[i + 1] for i in range(0, len(terms), 2)]
    return terms[0]


def factor_block(a):
    sub = lax.broadcasted_iota(jnp.int32, (8, H), 0)
    lane = lax.broadcasted_iota(jnp.int32, (8, H), 1)
    count = H // 8
    tiles = [[a[8 * t : 8 * t + 8, :], (lane == sub + 8 * t).astype(F32)] for t in range(count)]
    factor, inverse = [], []
    for t in range(count):
        j = 8 * t
        left, right = tiles[t]
        column = [spread_column(left, j + k) for k in range(8)]
        if t + 1 < count:
            following = [spread_column(tiles[t + 1][0], j + k) for k in range(8)]
        frow = jnp.zeros((8, H), F32)
        irow = jnp.zeros((8, H), F32)
        for p in range(8):
            here = sub == p
            pivot = spread_row(column[p], p)
            inv = 1.0 / pivot
            root = lax.rsqrt(pivot)

            signed = jnp.where(here, -1.0, column[p])

            def eliminate(z):
                return jnp.where(here, 0.0, z) - (signed * spread_row(z, p)) * inv

            frow = jnp.where(here, left * root, frow)
            irow = jnp.where(here, right * root, irow)
            for k in range(p + 1, 8):
                column[k] = eliminate(column[k])
            left, right = eliminate(left), eliminate(right)
        factor.append(jnp.where(lane >= sub + j, frow, 0.0))
        inverse.append(irow)
        if t + 1 < count:
            nxt = [
                old - tree([following[p] * spread_row(new, p) for p in range(8)])
                for old, new in zip(tiles[t + 1], (left, right))
            ]
            if t + 2 < count:
                below = jnp.concatenate([tiles[u][0] for u in range(t + 2, count)], 0)
                parts = [jnp.concatenate([left, right], 1)]
                if j:
                    parts = [jnp.zeros((j, 2 * H), F32)] + parts
                parts.append(jnp.zeros((H - 8 - j, 2 * H), F32))
                change = nn3_stacked(below, jnp.concatenate(parts, 0))
                for u in range(t + 2, count):
                    rows = change[8 * (u - t - 2) : 8 * (u - t - 1)]
                    tiles[u] = [tiles[u][0] - rows[:, :H], tiles[u][1] - rows[:, H:]]
            tiles[t + 1] = nxt
    return jnp.concatenate(factor, 0), jnp.concatenate(inverse, 0)


def kernel(
    rows_hbm, parent_hbm, map_hbm, leaf_hbm, prow_hbm, lf_out, pf_out,
    rows_ref, parent_ref, map_ref, xs, ps, hh, hl, gram, far, near, direct,
    work, diag, rleaf, rpar, slots,
    load_sem, small_sem, direct_send, direct_recv, far_send, far_recv, near_send, near_recv,
    lf_send, lf_recv, slot_send, slot_recv, pf_send, pf_recv,
):
    r = lax.axis_index("row")
    l = lax.axis_index("leaf")
    leaves = lax.axis_size("leaf")
    core = lax.rem(l, 2)
    live_rows = xs.shape[1]
    pieces = load_sem.shape[1]
    piece = live_rows // pieces

    def mod4(v):
        return lax.rem(v + 8, 4)

    place = [mod4(r - (2 * core + k)) for k in range(2)]
    first = jnp.where(jnp.logical_or(place[0] == 0, place[0] == 3), 1, 0)
    rp = 3 - 2 * core
    place.append(mod4(r - rp))
    k_mine = r - 2 * core
    factors = jnp.logical_and(k_mine >= 0, k_mine < 2)
    k_here = jnp.clip(k_mine, 0, 1)

    barrier = pltpu.get_barrier_semaphore()
    for step in (1, 2, 3):
        pl.semaphore_signal(barrier, inc=1, device_id={"row": mod4(r + step)}, device_id_type=MESH)
    greeted = 3
    for delta in (-2, -1, 1, 2):
        there = jnp.logical_and(l + delta >= 0, l + delta < leaves)

        @pl.when(there)
        def _(delta=delta):
            pl.semaphore_signal(barrier, inc=1, device_id={"leaf": l + delta}, device_id_type=MESH)

        greeted = greeted + jnp.where(there, 1, 0)

    def load(step, c):
        k = first if step == 0 else 1 - first
        part = pl.ds(c * piece, piece)
        return pltpu.make_async_copy(leaf_hbm.at[k, part], xs.at[k, part], load_sem.at[step, c])

    small = [
        pltpu.make_async_copy(rows_hbm, rows_ref, small_sem.at[0]),
        pltpu.make_async_copy(parent_hbm, parent_ref, small_sem.at[1]),
        pltpu.make_async_copy(map_hbm, map_ref, small_sem.at[2]),
        pltpu.make_async_copy(prow_hbm.at[0], ps, small_sem.at[3]),
    ]
    small[0].start()
    for step in range(2):
        for c in range(pieces):
            load(step, c).start()
    for copy in small[1:]:
        copy.start()

    def direct_copy(u):
        return pltpu.make_async_remote_copy(
            src_ref=gram.at[u, 0],
            dst_ref=direct.at[u],
            send_sem=direct_send.at[u],
            recv_sem=direct_recv.at[u],
            device_id={"row": mod4(r + 2)},
            device_id_type=MESH,
        )

    def far_copy(u, ci, side):
        b0, b1 = CHUNKS[ci]
        return pltpu.make_async_remote_copy(
            src_ref=gram.at[u, b0:b1, pl.ds(64 * side, 64)],
            dst_ref=far.at[u, b0:b1],
            send_sem=far_send.at[u, side, ci],
            recv_sem=far_recv.at[u, ci],
            device_id={"row": mod4(r - 1 + 2 * side)},
            device_id_type=MESH,
        )

    def near_copy(u, ci, side):
        b0, b1 = CHUNKS[ci] if ci >= 0 else (0, 1)
        return pltpu.make_async_remote_copy(
            src_ref=gram.at[u, b0:b1],
            dst_ref=near.at[u, side, b0:b1],
            send_sem=near_send.at[u, ci + 1],
            recv_sem=near_recv.at[u, side, ci + 1],
            device_id={"row": mod4(r - 1 + 2 * side)},
            device_id_type=MESH,
        )

    def start_first(u):
        @pl.when(place[u] == 2)
        def _():
            direct_copy(u).start()
            for side in range(2):
                far_copy(u, 0, side).start()

        for side in range(2):

            @pl.when(place[u] == 1 + 2 * side)
            def _(side=side):
                near_copy(u, -1, side).start()

    def next_far(u, ci):
        @pl.when(place[u] == 2)
        def _():
            for side in range(2):
                far_copy(u, ci - 1, side).wait_send()
                far_copy(u, ci, side).start()

    def forward(u, which, waits):
        for side in range(2):

            @pl.when(place[u] == 1 + 2 * side)
            def _(side=side):
                for ci in which:
                    b0, b1 = CHUNKS[ci]
                    far_copy(u, ci, side).wait_recv()
                    half = pl.ds(64 * side, 64)
                    gram[u, b0:b1, half] = gram[u, b0:b1, half] + far[u, b0:b1]
                    if ci == 1:

                        @pl.when(waits)
                        def _():
                            near_copy(u, 0, side).wait_send()

                    if ci == 2:

                        @pl.when(jnp.logical_not(waits))
                        def _():
                            near_copy(u, 0, side).wait_send()

                        near_copy(u, 1, side).wait_send()
                    near_copy(u, ci, side).start()

    def wait_near(u, ci):
        if ci < 0:
            direct_copy(u).wait_recv()
        for side in range(2):
            near_copy(u, ci, side).wait_recv()

    def drain(u):
        @pl.when(place[u] == 2)
        def _():
            direct_copy(u).wait_send()
            for side in range(2):
                far_copy(u, 2, side).wait_send()

        for side in range(2):

            @pl.when(place[u] == 1 + 2 * side)
            def _(side=side):
                for ci in (-1, 2):
                    near_copy(u, ci, side).wait_send()

    def summed(u, b):
        return gram[u, b] + (near[u, 0, b] + near[u, 1, b])

    def add_gram(x, start):
        high, low = split(x)
        for ref, rows, columns, other in (
            (hh, slice(0, 256), slice(0, N), high),
            (hh, slice(256, N), slice(256, N), high),
            (hl, slice(0, N), slice(0, N), low),
        ):
            value = tn(high[:, rows], other[:, columns])
            ref[rows, columns] = value if start else ref[rows, columns] + value

    def finish_gram(u, scale):
        for b, (i, j) in enumerate(BLOCKS):
            rows, columns = slice(H * i, H * i + H), slice(H * j, H * j + H)
            gram[u, b] = (hh[rows, columns] + (hl[rows, columns] + hl[columns, rows].T)) * scale

    total = 4 * live_rows
    small[0].wait()
    for step in range(2):
        k = first if step == 0 else 1 - first
        live = rows_ref[k] - r * live_rows
        for c in range(pieces):
            load(step, c).wait()
            x = xs[k, pl.ds(c * piece, piece)]
            position = lax.broadcasted_iota(jnp.int32, (piece, N), 0) + c * piece
            add_gram(jnp.where(position < live, x, 0.0), c == 0)
            if step == 1 and c < 2:
                for u in range(2):
                    next_far(u, c + 1)
        finish_gram(k, 1.0 / total)
        if step == 0:
            pl.semaphore_wait(barrier, greeted)
        for u in range(2):

            @pl.when(k == u)
            def _(u=u):
                start_first(u)

    for u in range(2):
        forward(u, (0, 1), jnp.logical_not(factors))

    def fill_rows(u, ci, add):
        wait_near(u, ci)
        b0, b1 = CHUNKS[ci]
        for b in range(b0, b1):
            i, j = BLOCKS[b]
            columns = slice(j * H, j * H + H)
            work[i, :, columns] = work[i, :, columns] + summed(u, b) if add else summed(u, b)

    def factor(u, count, out, beside, after):
        wait_near(u, -1)
        diag[...] = summed(u, 0) + direct[u]
        for b in range(count):
            diagonal, inverse = factor_block(diag[...])
            out[b, b] = diagonal
            beside(b)
            if b < 3:
                if b == 0:
                    fill_rows(u, 0, False)
                    fill_rows(u, 1, False)
                if b == 1:
                    fill_rows(u, 2, True)
                lo = b * H + H
                ih, il = split(inverse)

                def solve(columns):
                    wh, wl = split(work[b, :, columns])
                    return nn(ih, wh) + (nn(ih, wl) + nn(il, wh))

                near_panel = solve(slice(lo, lo + H))
                nh, nl = split(near_panel)
                out[b, b + 1] = near_panel
                if b == 0:
                    diag[...] = work[1, :, lo : lo + H] - tn3(nh, nl, nh, nl)
                else:
                    diag[...] = work[b + 1, :, lo : lo + H] - tn3(nh, nl, nh, nl)
                if b < 2:
                    rest = solve(slice(lo + H, N))
                    rh, rl = split(rest)
                    for q in range(b + 2, 4):
                        out[b, q] = rest[:, (q - b - 2) * H : (q - b - 1) * H]
                    columns = slice(lo + H, N)
                    work[b + 1, :, columns] = work[b + 1, :, columns] - tn3(nh, nl, rh, rl)
                    for i in range(b + 2, 4):
                        o = (i - b - 2) * H
                        columns = slice(i * H, N)
                        taken = tn3(rh[:, o : o + H], rl[:, o : o + H], rh[:, o:], rl[:, o:])
                        work[i, :, columns] = -taken if b == 0 else work[i, :, columns] - taken
            after(b)

    def lf_copy(k, b, q):
        return pltpu.make_async_remote_copy(
            src_ref=rleaf.at[b, q],
            dst_ref=lf_out.at[k, pl.ds(b * H, H)],
            send_sem=lf_send.at[b, q],
            recv_sem=lf_recv.at[k, b],
            device_id={"row": q},
            device_id_type=MESH,
        )

    def slot_copy(delta):
        return pltpu.make_async_remote_copy(
            src_ref=slots.at[2],
            dst_ref=slots.at[2 + delta],
            send_sem=slot_send.at[2 + delta],
            recv_sem=slot_recv.at[2 + delta],
            device_id={"leaf": l + delta},
            device_id_type=MESH,
        )

    sibling = l + 1 - 2 * core
    onward = 4 * core - 2

    def slot_copy(source, slot, device, send):
        return pltpu.make_async_remote_copy(
            src_ref=slots.at[source],
            dst_ref=slots.at[slot],
            send_sem=slot_send.at[send],
            recv_sem=slot_recv.at[slot],
            device_id={"leaf": device},
            device_id_type=MESH,
        )

    def inside(place_of):
        return jnp.logical_and(place_of >= 0, place_of < leaves)

    def own_slot(delta):
        return slot_copy(2, 2 + delta, l + delta, 2 + delta)

    def sibling_slot():
        return slot_copy(2, 2 + sibling - l, sibling, 1)

    def onward_slot():
        return slot_copy(2 + onward, 1 + 2 * core, sibling, 2)

    @pl.when(factors)
    def _():
        def beside(b):
            if b == 0:
                for u in range(2):
                    forward(u, (2,), jnp.logical_not(factors))

        factor(k_here, 2, rleaf, beside, lambda b: None)
        slots[2, 0] = diag[...]
        slots[2, 1] = work[2, :, 384:N]
        slots[2, 2] = work[3, :, 384:N]
        for delta in (-2, 2):

            @pl.when(inside(l + delta))
            def _(delta=delta):
                own_slot(delta).start()

        sibling_slot().start()
    @pl.when(jnp.logical_not(factors))
    def _():
        for u in range(2):
            forward(u, (2,), jnp.logical_not(factors))

    for copy in small[1:]:
        copy.wait()
    add_gram(ps[...], True)
    finish_gram(2, 1.0 / (4 * ps.shape[0]))
    for k in range(2):

        @pl.when(r == 0)
        def _(k=k):
            lf_out[k, H : 2 * H] = jnp.zeros((H, H), F32)

    for b in range(1, 4):

        @pl.when(b > r)
        def _(b=b):
            pf_out[0, b * H : b * H + H] = jnp.zeros((H, H), F32)

    @pl.when(factors)
    def _():
        for q in range(4):
            for b in range(min(q, 1) + 1):

                @pl.when(q != r)
                def _(q=q, b=b):
                    lf_copy(k_here, b, q).start()

                @pl.when(q == r)
                def _(q=q, b=b):
                    lf_out[k_here, b * H : b * H + H] = rleaf[b, q]

    def place_slot(i, carry):
        one = 2 * core - 1
        delta = jnp.where(
            factors,
            jnp.where(i == 0, 0, jnp.where(i == 1, onward, -onward)),
            jnp.where(i == 0, one, -one),
        )
        source = l - delta
        valid = jnp.logical_and(jnp.logical_or(factors, i < 2), inside(source))

        @pl.when(valid)
        def _():
            slot = 2 + delta

            @pl.when(delta != 0)
            def _():
                slot_copy(2, slot, sibling, 0).wait_recv()

            @pl.when(jnp.logical_and(factors, i == 1))
            def _():
                onward_slot().start()

            front = 2 * source + lax.rem(r, 2)
            away = jnp.where(parent_ref[front] == l, 0, 2 * N)
            target = map_ref[pl.ds(front, 1), :] + away
            chosen = (lax.broadcasted_iota(jnp.int32, (N, 256), 0) == target).astype(F32).astype(BF16)
            s = slots[slot]
            square = jnp.concatenate(
                [jnp.concatenate([s[0], s[1]], 1), jnp.concatenate([s[1].T, s[2]], 1)], 0
            )
            high, low = split(square)
            high_rows, low_rows = nn(chosen, high).astype(BF16), nn(chosen, low).astype(BF16)
            for half in range(2):
                rows, columns = slice(256 * half, 256 * half + 256), slice(256 * half, N)
                placed = nt(high_rows[rows], chosen[columns]) + nt(low_rows[rows], chosen[columns])
                for b, (bi, bj) in enumerate(BLOCKS):
                    if bi // 2 == half:
                        ii, jj = (bi - 2 * half) * H, (bj - 2 * half) * H
                        gram[2, b] = gram[2, b] + placed[ii : ii + H, jj : jj + H]

        return carry

    lax.fori_loop(0, 3, place_slot, 0)

    start_first(2)
    for ci in (1, 2):
        next_far(2, ci)
    forward(2, (0, 1, 2), l >= 0)

    def pf_copy(b, q):
        return pltpu.make_async_remote_copy(
            src_ref=rpar.at[b, q],
            dst_ref=pf_out.at[0, pl.ds(b * H, H)],
            send_sem=pf_send.at[b, q],
            recv_sem=pf_recv.at[b],
            device_id={"row": q},
            device_id_type=MESH,
        )

    @pl.when(place[2] == 0)
    def _():
        def after(b):
            for q in range(b, 4):

                @pl.when(q != r)
                def _(q=q):
                    pf_copy(b, q).start()

                @pl.when(q == r)
                def _(q=q):
                    pf_out[0, b * H : b * H + H] = rpar[b, q]

        factor(2, 4, rpar, lambda b: None, after)
        for q in range(4):

            @pl.when(q != r)
            def _(q=q):
                for b in range(q + 1):
                    pf_copy(b, q).wait_send()

    @pl.when(place[2] != 0)
    def _():
        for b in range(4):

            @pl.when(b <= r)
            def _(b=b):
                pf_copy(b, 0).wait_recv()

    for k in range(2):

        @pl.when(k_mine != k)
        def _(k=k):
            lf_copy(k, 0, 0).wait_recv()

            @pl.when(r > 0)
            def _():
                lf_copy(k, 1, 0).wait_recv()

        @pl.when(k_mine == k)
        def _(k=k):
            for q in range(4):

                @pl.when(q != r)
                def _(q=q):
                    for b in range(min(q, 1) + 1):
                        lf_copy(k, b, q).wait_send()

    @pl.when(factors)
    def _():
        for delta in (-2, 2):

            @pl.when(inside(l + delta))
            def _(delta=delta):
                own_slot(delta).wait_send()

        sibling_slot().wait_send()

        @pl.when(inside(l - onward))
        def _():
            onward_slot().wait_send()

    for u in range(3):
        drain(u)


def per_device(leaf_fronts, front_rows, parent_of, column_map, parent_rows):
    kids, live_rows, _ = leaf_fronts.shape
    chunks = len(CHUNKS)
    dma = pltpu.SemaphoreType.DMA
    vmem = pltpu.VMEM
    return pl.pallas_call(
        kernel,
        out_shape=(
            jax.ShapeDtypeStruct((kids, 256, H), F32),
            jax.ShapeDtypeStruct((1, N, H), F32),
        ),
        in_specs=[pl.BlockSpec(memory_space=pltpu.HBM)] * 5,
        out_specs=(pl.BlockSpec(memory_space=pltpu.VMEM),) * 2,
        scratch_shapes=[
            pltpu.SMEM(front_rows.shape, jnp.int32),
            pltpu.SMEM(parent_of.shape, jnp.int32),
            vmem(column_map.shape, jnp.int32),
            vmem((kids, live_rows, N), F32),
            vmem(parent_rows.shape[1:], F32),
            vmem((N, N), F32),
            vmem((N, N), F32),
            vmem((3, 10, H, H), F32),
            vmem((3, 10, H // 2, H), F32),
            vmem((3, 2, 10, H, H), F32),
            vmem((3, H, H), F32),
            vmem((4, H, N), F32),
            vmem((H, H), F32),
            vmem((2, 4, H, H), F32),
            vmem((4, 4, H, H), F32),
            vmem((5, 3, H, H), F32),
            dma((2, 2)),
            dma((4,)),
            dma((3,)),
            dma((3,)),
            dma((3, 2, chunks)),
            dma((3, chunks)),
            dma((3, chunks + 1)),
            dma((3, 2, chunks + 1)),
            dma((2, 4)),
            dma((2, 2)),
            dma((5,)),
            dma((5,)),
            dma((4, 4)),
            dma((4,)),
        ],
        compiler_params=pltpu.CompilerParams(
            collective_id=0, has_side_effects=True, vmem_limit_bytes=60 << 20
        ),
        name="fronts",
    )(front_rows, parent_of, column_map, leaf_fronts, parent_rows)


def solution(mesh):
    return jax.shard_map(
        per_device,
        mesh=mesh,
        in_specs=(P("leaf", "row", None), P("leaf"), P(), P(), P("leaf", "row", None)),
        out_specs=(P("leaf", None, "row"), P("leaf", None, "row")),
        check_vma=False,
    )
```

```python
import jax
import jax.numpy as jnp
from jax import lax
from jax.experimental import pallas as pl
from jax.experimental.pallas import tpu as pltpu
from jax.sharding import PartitionSpec as P

F32, BF16 = jnp.float32, jnp.bfloat16
MESH = pl.DeviceIdType.MESH
N = 512
H = 128
BLOCKS = [(i, j) for i in range(4) for j in range(i, 4)]
CHUNKS = ((1, 5), (5, 7), (7, 10))
REACH = 2


def split(x):
    high = x.astype(BF16)
    return high, (x - high.astype(F32)).astype(BF16)


def nn(a, b):
    return jnp.dot(a, b, preferred_element_type=F32)


def tn(a, b):
    return lax.dot_general(a, b, (((0,), (0,)), ((), ())), preferred_element_type=F32)


def nt(a, b):
    return lax.dot_general(a, b, (((1,), (1,)), ((), ())), preferred_element_type=F32)


def nn3(a, b):
    ah, al = split(a)
    bh, bl = split(b)
    return nn(ah, bh) + (nn(ah, bl) + nn(al, bh))


def nn3_stacked(a, b):
    ah, al = split(a)
    bh, bl = split(b)
    return nn(jnp.concatenate([ah, al, ah], 1), jnp.concatenate([bh, bh, bl], 0))


def tn3(ah, al, bh, bl):
    return tn(ah, bh) + (tn(ah, bl) + tn(al, bh))


def spread_row(x, p):
    return jnp.broadcast_to(x[p : p + 1, :], (8, H))


def spread_column(x, k):
    return jnp.take_along_axis(x, jnp.full((8, H), k, jnp.int32), axis=1)


def tree(terms):
    while len(terms) > 1:
        terms = [terms[i] + terms[i + 1] for i in range(0, len(terms), 2)]
    return terms[0]


def factor_block(a):
    sub = lax.broadcasted_iota(jnp.int32, (8, H), 0)
    lane = lax.broadcasted_iota(jnp.int32, (8, H), 1)
    count = H // 8
    tiles = [[a[8 * t : 8 * t + 8, :], (lane == sub + 8 * t).astype(F32)] for t in range(count)]
    factor, inverse = [], []
    for t in range(count):
        j = 8 * t
        left, right = tiles[t]
        column = [spread_column(left, j + k) for k in range(8)]
        if t + 1 < count:
            following = [spread_column(tiles[t + 1][0], j + k) for k in range(8)]
        frow = jnp.zeros((8, H), F32)
        irow = jnp.zeros((8, H), F32)
        for p in range(8):
            here = sub == p
            pivot = spread_row(column[p], p)
            inv = 1.0 / pivot
            root = lax.rsqrt(pivot)

            signed = jnp.where(here, -1.0, column[p])

            def eliminate(z):
                return jnp.where(here, 0.0, z) - (signed * spread_row(z, p)) * inv

            frow = jnp.where(here, left * root, frow)
            irow = jnp.where(here, right * root, irow)
            for k in range(p + 1, 8):
                column[k] = eliminate(column[k])
            left, right = eliminate(left), eliminate(right)
        factor.append(jnp.where(lane >= sub + j, frow, 0.0))
        inverse.append(irow)
        if t + 1 < count:
            nxt = [
                old - tree([following[p] * spread_row(new, p) for p in range(8)])
                for old, new in zip(tiles[t + 1], (left, right))
            ]
            if t + 2 < count:
                below = jnp.concatenate([tiles[u][0] for u in range(t + 2, count)], 0)
                parts = [jnp.concatenate([left, right], 1)]
                if j:
                    parts = [jnp.zeros((j, 2 * H), F32)] + parts
                parts.append(jnp.zeros((H - 8 - j, 2 * H), F32))
                change = nn3_stacked(below, jnp.concatenate(parts, 0))
                for u in range(t + 2, count):
                    rows = change[8 * (u - t - 2) : 8 * (u - t - 1)]
                    tiles[u] = [tiles[u][0] - rows[:, :H], tiles[u][1] - rows[:, H:]]
            tiles[t + 1] = nxt
    return jnp.concatenate(factor, 0), jnp.concatenate(inverse, 0)


def kernel(
    rows_hbm, parent_hbm, map_hbm, leaf_hbm, prow_hbm, lf_out, pf_out,
    rows_ref, parent_ref, map_ref, xs, ps, hh, hl, gram, far, near, direct,
    work, diag, rleaf, rpar, slots,
    load_sem, small_sem, direct_send, direct_recv, far_send, far_recv, near_send, near_recv,
    lf_send, lf_recv, slot_send, slot_recv, pf_send, pf_recv,
):
    r = lax.axis_index("row")
    l = lax.axis_index("leaf")
    leaves = lax.axis_size("leaf")
    core = lax.rem(l, 2)
    live_rows = xs.shape[1]
    pieces = load_sem.shape[1]
    piece = live_rows // pieces

    def mod4(v):
        return lax.rem(v + 8, 4)

    place = [mod4(r - (2 * core + k)) for k in range(2)]
    first = jnp.where(jnp.logical_or(place[0] == 0, place[0] == 3), 1, 0)
    rp = core
    place.append(mod4(r - rp))
    k_mine = r - 2 * core
    factors = jnp.logical_and(k_mine >= 0, k_mine < 2)
    k_here = jnp.clip(k_mine, 0, 1)

    barrier = pltpu.get_barrier_semaphore()
    for step in (1, 2, 3):
        pl.semaphore_signal(barrier, inc=1, device_id={"row": mod4(r + step)}, device_id_type=MESH)
    greeted = 3
    for delta in (-2, -1, 1, 2):
        there = jnp.logical_and(l + delta >= 0, l + delta < leaves)

        @pl.when(there)
        def _(delta=delta):
            pl.semaphore_signal(barrier, inc=1, device_id={"leaf": l + delta}, device_id_type=MESH)

        greeted = greeted + jnp.where(there, 1, 0)

    def load(step, c):
        k = first if step == 0 else 1 - first
        part = pl.ds(c * piece, piece)
        return pltpu.make_async_copy(leaf_hbm.at[k, part], xs.at[k, part], load_sem.at[step, c])

    small = [
        pltpu.make_async_copy(rows_hbm, rows_ref, small_sem.at[0]),
        pltpu.make_async_copy(parent_hbm, parent_ref, small_sem.at[1]),
        pltpu.make_async_copy(map_hbm, map_ref, small_sem.at[2]),
        pltpu.make_async_copy(prow_hbm.at[0], ps, small_sem.at[3]),
    ]
    small[0].start()
    for step in range(2):
        for c in range(pieces):
            load(step, c).start()
    for copy in small[1:]:
        copy.start()

    def direct_copy(u):
        return pltpu.make_async_remote_copy(
            src_ref=gram.at[u, 0],
            dst_ref=direct.at[u],
            send_sem=direct_send.at[u],
            recv_sem=direct_recv.at[u],
            device_id={"row": mod4(r + 2)},
            device_id_type=MESH,
        )

    def far_copy(u, ci, side):
        b0, b1 = CHUNKS[ci]
        return pltpu.make_async_remote_copy(
            src_ref=gram.at[u, b0:b1, pl.ds(64 * side, 64)],
            dst_ref=far.at[u, b0:b1],
            send_sem=far_send.at[u, side, ci],
            recv_sem=far_recv.at[u, ci],
            device_id={"row": mod4(r - 1 + 2 * side)},
            device_id_type=MESH,
        )

    def near_copy(u, ci, side):
        b0, b1 = CHUNKS[ci] if ci >= 0 else (0, 1)
        return pltpu.make_async_remote_copy(
            src_ref=gram.at[u, b0:b1],
            dst_ref=near.at[u, side, b0:b1],
            send_sem=near_send.at[u, ci + 1],
            recv_sem=near_recv.at[u, side, ci + 1],
            device_id={"row": mod4(r - 1 + 2 * side)},
            device_id_type=MESH,
        )

    def start_first(u):
        @pl.when(place[u] == 2)
        def _():
            direct_copy(u).start()
            for side in range(2):
                far_copy(u, 0, side).start()

        for side in range(2):

            @pl.when(place[u] == 1 + 2 * side)
            def _(side=side):
                near_copy(u, -1, side).start()

    def next_far(u, ci):
        @pl.when(place[u] == 2)
        def _():
            for side in range(2):
                far_copy(u, ci, side).start()

    def forward(u, which, waits):
        for side in range(2):

            @pl.when(place[u] == 1 + 2 * side)
            def _(side=side):
                for ci in which:
                    b0, b1 = CHUNKS[ci]
                    far_copy(u, ci, side).wait_recv()
                    half = pl.ds(64 * side, 64)
                    gram[u, b0:b1, half] = gram[u, b0:b1, half] + far[u, b0:b1]
                    if waits and ci:
                        near_copy(u, ci - 2, side).wait_send()
                    near_copy(u, ci, side).start()

    def wait_near(u, ci):
        if ci < 0:
            direct_copy(u).wait_recv()
        for side in range(2):
            near_copy(u, ci, side).wait_recv()

    def drain(u):
        @pl.when(place[u] == 2)
        def _():
            direct_copy(u).wait_send()
            for ci in range(len(CHUNKS)):
                for side in range(2):
                    far_copy(u, ci, side).wait_send()

        for side in range(2):

            @pl.when(place[u] == 1 + 2 * side)
            def _(side=side):
                for ci in (1, 2) if u == 2 else range(-1, 3):
                    near_copy(u, ci, side).wait_send()

    def summed(u, b):
        return gram[u, b] + (near[u, 0, b] + near[u, 1, b])

    def add_gram(x, start):
        high, low = split(x)
        for ref, rows, columns, other in (
            (hh, slice(0, 256), slice(0, N), high),
            (hh, slice(256, N), slice(256, N), high),
            (hl, slice(0, N), slice(0, N), low),
        ):
            value = tn(high[:, rows], other[:, columns])
            ref[rows, columns] = value if start else ref[rows, columns] + value

    def finish_gram(u, scale):
        for b, (i, j) in enumerate(BLOCKS):
            rows, columns = slice(H * i, H * i + H), slice(H * j, H * j + H)
            gram[u, b] = (hh[rows, columns] + (hl[rows, columns] + hl[columns, rows].T)) * scale

    total = 4 * live_rows
    small[0].wait()
    for step in range(2):
        k = first if step == 0 else 1 - first
        live = rows_ref[k] - r * live_rows
        for c in range(pieces):
            load(step, c).wait()
            x = xs[k, pl.ds(c * piece, piece)]
            position = lax.broadcasted_iota(jnp.int32, (piece, N), 0) + c * piece
            add_gram(jnp.where(position < live, x, 0.0), c == 0)
            if step == 1 and c < 2:
                for u in range(2):
                    next_far(u, c + 1)
        finish_gram(k, 1.0 / total)
        if step == 0:
            pl.semaphore_wait(barrier, greeted)
        for u in range(2):

            @pl.when(k == u)
            def _(u=u):
                start_first(u)

    for u in range(2):
        forward(u, (0, 1), False)

    def fill_rows(u, ci):
        wait_near(u, ci)
        add = ci > 0
        b0, b1 = CHUNKS[ci]
        for b in range(b0, b1):
            i, j = BLOCKS[b]
            columns = slice(j * H, j * H + H)
            work[i, :, columns] = work[i, :, columns] + summed(u, b) if add else summed(u, b)

    def factor(u, count, out, beside, after):
        wait_near(u, -1)
        diag[...] = summed(u, 0) + direct[u]
        for b in range(count):
            diagonal, inverse = factor_block(diag[...])
            out[b, b] = diagonal
            beside(b)
            if b < 3:
                if b == 0:
                    fill_rows(u, 0)
                if b == 1:
                    fill_rows(u, 1)
                    fill_rows(u, 2)
                lo = b * H + H
                ih, il = split(inverse)

                def solve(columns):
                    wh, wl = split(work[b, :, columns])
                    return nn(ih, wh) + (nn(ih, wl) + nn(il, wh))

                near_panel = solve(slice(lo, lo + H))
                nh, nl = split(near_panel)
                out[b, b + 1] = near_panel
                diag[...] = work[b + 1, :, lo : lo + H] - tn3(nh, nl, nh, nl)
                if b < 2:
                    rest = solve(slice(lo + H, N))
                    rh, rl = split(rest)
                    for q in range(b + 2, 4):
                        out[b, q] = rest[:, (q - b - 2) * H : (q - b - 1) * H]
                    columns = slice(lo + H, N)
                    taken = tn3(nh, nl, rh, rl)
                    work[b + 1, :, columns] = -taken if b == 0 else work[b + 1, :, columns] - taken
                    for i in range(b + 2, 4):
                        o = (i - b - 2) * H
                        columns = slice(i * H, N)
                        taken = tn3(rh[:, o : o + H], rl[:, o : o + H], rh[:, o:], rl[:, o:])
                        work[i, :, columns] = -taken if b == 0 else work[i, :, columns] - taken
            after(b)

    def lf_copy(k, b, q):
        return pltpu.make_async_remote_copy(
            src_ref=rleaf.at[b, q],
            dst_ref=lf_out.at[k, pl.ds(b * H, H)],
            send_sem=lf_send.at[b, q],
            recv_sem=lf_recv.at[k, b],
            device_id={"row": q},
            device_id_type=MESH,
        )

    def slot_copy(delta):
        return pltpu.make_async_remote_copy(
            src_ref=slots.at[2],
            dst_ref=slots.at[2 + delta],
            send_sem=slot_send.at[2 + delta],
            recv_sem=slot_recv.at[2 + delta],
            device_id={"leaf": l + delta},
            device_id_type=MESH,
        )

    sibling = l + 1 - 2 * core
    onward = 4 * core - 2

    def slot_copy(source, slot, device, send):
        return pltpu.make_async_remote_copy(
            src_ref=slots.at[source],
            dst_ref=slots.at[slot],
            send_sem=slot_send.at[send],
            recv_sem=slot_recv.at[slot],
            device_id={"leaf": device},
            device_id_type=MESH,
        )

    def inside(place_of):
        return jnp.logical_and(place_of >= 0, place_of < leaves)

    def own_slot(delta):
        return slot_copy(2, 2 + delta, l + delta, 2 + delta)

    def sibling_slot():
        return slot_copy(2, 2 + sibling - l, sibling, 1)

    def onward_slot():
        return slot_copy(2 + onward, 1 + 2 * core, sibling, 2)

    @pl.when(factors)
    def _():
        def beside(b):
            if b == 0:
                for u in range(2):
                    forward(u, (2,), False)

        factor(k_here, 2, rleaf, beside, lambda b: None)
        slots[2, 0] = diag[...]
        slots[2, 1] = work[2, :, 384:N]
        slots[2, 2] = work[3, :, 384:N]
        for delta in (-2, 2):

            @pl.when(inside(l + delta))
            def _(delta=delta):
                own_slot(delta).start()

        sibling_slot().start()
    @pl.when(jnp.logical_not(factors))
    def _():
        for u in range(2):
            forward(u, (2,), False)

    for copy in small[1:]:
        copy.wait()
    add_gram(ps[...], True)
    finish_gram(2, 1.0 / (4 * ps.shape[0]))
    for k in range(2):

        @pl.when(r == 0)
        def _(k=k):
            lf_out[k, H : 2 * H] = jnp.zeros((H, H), F32)

    for b in range(1, 4):

        @pl.when(b > r)
        def _(b=b):
            pf_out[0, b * H : b * H + H] = jnp.zeros((H, H), F32)

    @pl.when(factors)
    def _():
        for q in range(4):
            for b in range(min(q, 1) + 1):

                @pl.when(q != r)
                def _(q=q, b=b):
                    lf_copy(k_here, b, q).start()

                @pl.when(q == r)
                def _(q=q, b=b):
                    lf_out[k_here, b * H : b * H + H] = rleaf[b, q]

    def place_slot(i, carry):
        one = 2 * core - 1
        delta = jnp.where(
            factors,
            jnp.where(i == 0, 0, jnp.where(i == 1, onward, -onward)),
            jnp.where(i == 0, one, -one),
        )
        source = l - delta
        valid = jnp.logical_and(jnp.logical_or(factors, i < 2), inside(source))

        @pl.when(valid)
        def _():
            slot = 2 + delta

            @pl.when(delta != 0)
            def _():
                slot_copy(2, slot, sibling, 0).wait_recv()

            @pl.when(jnp.logical_and(factors, i == 1))
            def _():
                onward_slot().start()

            front = 2 * source + lax.rem(r, 2)
            away = jnp.where(parent_ref[front] == l, 0, 2 * N)
            target = map_ref[pl.ds(front, 1), :] + away
            chosen = (lax.broadcasted_iota(jnp.int32, (N, 256), 0) == target).astype(F32).astype(BF16)
            s = slots[slot]
            square = jnp.concatenate(
                [jnp.concatenate([s[0], s[1]], 1), jnp.concatenate([s[1].T, s[2]], 1)], 0
            )
            high, low = split(square)
            high_rows, low_rows = nn(chosen, high).astype(BF16), nn(chosen, low).astype(BF16)
            for half in range(2):
                rows, columns = slice(256 * half, 256 * half + 256), slice(256 * half, N)
                placed = nt(high_rows[rows], chosen[columns]) + nt(low_rows[rows], chosen[columns])
                for b, (bi, bj) in enumerate(BLOCKS):
                    if bi // 2 == half:
                        ii, jj = (bi - 2 * half) * H, (bj - 2 * half) * H
                        gram[2, b] = gram[2, b] + placed[ii : ii + H, jj : jj + H]

        return carry

    lax.fori_loop(0, 3, place_slot, 0)

    start_first(2)
    for ci in (1, 2):
        next_far(2, ci)
    forward(2, (0, 1, 2), True)

    def pf_copy(b, q):
        return pltpu.make_async_remote_copy(
            src_ref=rpar.at[b, q],
            dst_ref=pf_out.at[0, pl.ds(b * H, H)],
            send_sem=pf_send.at[b, q],
            recv_sem=pf_recv.at[b],
            device_id={"row": q},
            device_id_type=MESH,
        )

    @pl.when(place[2] == 0)
    def _():
        def after(b):
            for q in range(b, 4):

                @pl.when(q != r)
                def _(q=q):
                    pf_copy(b, q).start()

                @pl.when(q == r)
                def _(q=q):
                    pf_out[0, b * H : b * H + H] = rpar[b, q]

        factor(2, 4, rpar, lambda b: None, after)
        for q in range(4):

            @pl.when(q != r)
            def _(q=q):
                for b in range(q + 1):
                    pf_copy(b, q).wait_send()

    @pl.when(place[2] != 0)
    def _():
        for b in range(4):

            @pl.when(b <= r)
            def _(b=b):
                pf_copy(b, 0).wait_recv()

    for k in range(2):

        @pl.when(k_mine != k)
        def _(k=k):
            lf_copy(k, 0, 0).wait_recv()

            @pl.when(r > 0)
            def _():
                lf_copy(k, 1, 0).wait_recv()

        @pl.when(k_mine == k)
        def _(k=k):
            for q in range(4):

                @pl.when(q != r)
                def _(q=q):
                    for b in range(min(q, 1) + 1):
                        lf_copy(k, b, q).wait_send()

    @pl.when(factors)
    def _():
        for delta in (-2, 2):

            @pl.when(inside(l + delta))
            def _(delta=delta):
                own_slot(delta).wait_send()

        sibling_slot().wait_send()

        @pl.when(inside(l - onward))
        def _():
            onward_slot().wait_send()

    for u in range(3):
        drain(u)


def hand_over(leaf_in, parent_in, leaf_out, parent_out, sems):
    copies = [
        pltpu.make_async_copy(source.at[part], target.at[part], sems.at[i, j])
        for i, (source, target, parts) in enumerate((
            (leaf_in, leaf_out, [(k, pl.ds(h * H, H)) for k in range(2) for h in range(2)]),
            (parent_in, parent_out, [(0, pl.ds(h * H, H)) for h in range(4)]),
        ))
        for j, part in enumerate(parts)
    ]
    for copy in copies:
        copy.start()
    for copy in copies:
        copy.wait()


def per_device(leaf_fronts, front_rows, parent_of, column_map, parent_rows):
    kids, live_rows, _ = leaf_fronts.shape
    chunks = len(CHUNKS)
    dma = pltpu.SemaphoreType.DMA
    vmem = pltpu.VMEM
    factors = pl.pallas_call(
        kernel,
        out_shape=(
            jax.ShapeDtypeStruct((kids, 256, H), F32),
            jax.ShapeDtypeStruct((1, N, H), F32),
        ),
        in_specs=[pl.BlockSpec(memory_space=pltpu.HBM)] * 5,
        out_specs=(pl.BlockSpec(memory_space=pltpu.VMEM),) * 2,
        scratch_shapes=[
            pltpu.SMEM(front_rows.shape, jnp.int32),
            pltpu.SMEM(parent_of.shape, jnp.int32),
            vmem(column_map.shape, jnp.int32),
            vmem((kids, live_rows, N), F32),
            vmem(parent_rows.shape[1:], F32),
            vmem((N, N), F32),
            vmem((N, N), F32),
            vmem((3, 10, H, H), F32),
            vmem((3, 10, H // 2, H), F32),
            vmem((3, 2, 10, H, H), F32),
            vmem((3, H, H), F32),
            vmem((4, H, N), F32),
            vmem((H, H), F32),
            vmem((2, 4, H, H), F32),
            vmem((4, 4, H, H), F32),
            vmem((5, 3, H, H), F32),
            dma((2, 2)),
            dma((4,)),
            dma((3,)),
            dma((3,)),
            dma((3, 2, chunks)),
            dma((3, chunks)),
            dma((3, chunks + 1)),
            dma((3, 2, chunks + 1)),
            dma((2, 4)),
            dma((2, 2)),
            dma((5,)),
            dma((5,)),
            dma((4, 4)),
            dma((4,)),
        ],
        compiler_params=pltpu.CompilerParams(
            collective_id=0, has_side_effects=True, vmem_limit_bytes=60 << 20
        ),
        name="fronts",
    )(front_rows, parent_of, column_map, leaf_fronts, parent_rows)
    hbm = pl.BlockSpec(memory_space=pltpu.HBM)
    return pl.pallas_call(
        hand_over,
        out_shape=[jax.ShapeDtypeStruct(x.shape, x.dtype) for x in factors],
        in_specs=[hbm] * 2,
        out_specs=[hbm] * 2,
        scratch_shapes=[dma((2, 4))],
        name="hand_over",
    )(*factors)


def solution(mesh):
    return jax.shard_map(
        per_device,
        mesh=mesh,
        in_specs=(P("leaf", "row", None), P("leaf"), P(), P(), P("leaf", "row", None)),
        out_specs=(P("leaf", None, "row"), P("leaf", None, "row")),
        check_vma=False,
    )
```

```python
import jax
import jax.numpy as jnp
from jax import lax
from jax.experimental import pallas as pl
from jax.experimental.pallas import tpu as pltpu
from jax.sharding import PartitionSpec as P

F32, BF16 = jnp.float32, jnp.bfloat16
MESH = pl.DeviceIdType.MESH
N = 512
H = 128
BLOCKS = [(i, j) for i in range(4) for j in range(i, 4)]
CHUNKS = ((1, 5), (5, 7), (7, 10))
REACH = 2


def split(x):
    high = x.astype(BF16)
    return high, (x - high.astype(F32)).astype(BF16)


def nn(a, b):
    return jnp.dot(a, b, preferred_element_type=F32)


def tn(a, b):
    return lax.dot_general(a, b, (((0,), (0,)), ((), ())), preferred_element_type=F32)


def nt(a, b):
    return lax.dot_general(a, b, (((1,), (1,)), ((), ())), preferred_element_type=F32)


def nn3(a, b):
    ah, al = split(a)
    bh, bl = split(b)
    return nn(ah, bh) + (nn(ah, bl) + nn(al, bh))


def nn3_stacked(a, b):
    ah, al = split(a)
    bh, bl = split(b)
    return nn(jnp.concatenate([ah, al, ah], 1), jnp.concatenate([bh, bh, bl], 0))


def tn3(ah, al, bh, bl):
    return tn(ah, bh) + (tn(ah, bl) + tn(al, bh))


def spread_row(x, p):
    return jnp.broadcast_to(x[p : p + 1, :], (8, H))


def spread_column(x, k):
    return jnp.take_along_axis(x, jnp.full((8, H), k, jnp.int32), axis=1)


def tree(terms):
    while len(terms) > 1:
        terms = [terms[i] + terms[i + 1] for i in range(0, len(terms), 2)]
    return terms[0]


def factor_block(a):
    sub = lax.broadcasted_iota(jnp.int32, (8, H), 0)
    lane = lax.broadcasted_iota(jnp.int32, (8, H), 1)
    count = H // 8
    tiles = [[a[8 * t : 8 * t + 8, :], (lane == sub + 8 * t).astype(F32)] for t in range(count)]
    factor, inverse = [], []
    for t in range(count):
        j = 8 * t
        left, right = tiles[t]
        column = [spread_column(left, j + k) for k in range(8)]
        if t + 1 < count:
            following = [spread_column(tiles[t + 1][0], j + k) for k in range(8)]
        frow = jnp.zeros((8, H), F32)
        irow = jnp.zeros((8, H), F32)
        for p in range(8):
            here = sub == p
            pivot = spread_row(column[p], p)
            inv = 1.0 / pivot
            root = lax.rsqrt(pivot)

            signed = jnp.where(here, -1.0, column[p])

            def eliminate(z):
                return jnp.where(here, 0.0, z) - (signed * spread_row(z, p)) * inv

            frow = jnp.where(here, left * root, frow)
            irow = jnp.where(here, right * root, irow)
            for k in range(p + 1, 8):
                column[k] = eliminate(column[k])
            left, right = eliminate(left), eliminate(right)
        factor.append(jnp.where(lane >= sub + j, frow, 0.0))
        inverse.append(irow)
        if t + 1 < count:
            nxt = [
                old - tree([following[p] * spread_row(new, p) for p in range(8)])
                for old, new in zip(tiles[t + 1], (left, right))
            ]
            if t + 2 < count:
                below = jnp.concatenate([tiles[u][0] for u in range(t + 2, count)], 0)
                parts = [jnp.concatenate([left, right], 1)]
                if j:
                    parts = [jnp.zeros((j, 2 * H), F32)] + parts
                parts.append(jnp.zeros((H - 8 - j, 2 * H), F32))
                change = nn3_stacked(below, jnp.concatenate(parts, 0))
                for u in range(t + 2, count):
                    rows = change[8 * (u - t - 2) : 8 * (u - t - 1)]
                    tiles[u] = [tiles[u][0] - rows[:, :H], tiles[u][1] - rows[:, H:]]
            tiles[t + 1] = nxt
    return jnp.concatenate(factor, 0), jnp.concatenate(inverse, 0)


def kernel(
    rows_hbm, parent_hbm, map_hbm, leaf_hbm, prow_hbm, lf_out, pf_out,
    rows_ref, parent_ref, map_ref, xs, ps, hh, hl, gram, far, near, direct,
    work, diag, rleaf, rpar, slots,
    load_sem, small_sem, direct_send, direct_recv, far_send, far_recv, near_send, near_recv,
    lf_send, lf_recv, slot_send, slot_recv, pf_send, pf_recv,
):
    r = lax.axis_index("row")
    l = lax.axis_index("leaf")
    leaves = lax.axis_size("leaf")
    core = lax.rem(l, 2)
    live_rows = xs.shape[1]
    pieces = load_sem.shape[1]
    piece = live_rows // pieces

    def mod4(v):
        return lax.rem(v + 8, 4)

    base = 2 - 2 * core
    place = [mod4(r - (base + k)) for k in range(2)]
    first = jnp.where(jnp.logical_or(place[0] == 0, place[0] == 3), 1, 0)
    rp = 3 - core
    place.append(mod4(r - rp))
    k_mine = r - base
    factors = jnp.logical_and(k_mine >= 0, k_mine < 2)
    k_here = jnp.clip(k_mine, 0, 1)

    barrier = pltpu.get_barrier_semaphore()
    for step in (1, 2, 3):
        pl.semaphore_signal(barrier, inc=1, device_id={"row": mod4(r + step)}, device_id_type=MESH)
    greeted = 3
    for delta in (-2, -1, 1, 2):
        there = jnp.logical_and(l + delta >= 0, l + delta < leaves)

        @pl.when(there)
        def _(delta=delta):
            pl.semaphore_signal(barrier, inc=1, device_id={"leaf": l + delta}, device_id_type=MESH)

        greeted = greeted + jnp.where(there, 1, 0)

    def load(step, c):
        k = first if step == 0 else 1 - first
        part = pl.ds(c * piece, piece)
        return pltpu.make_async_copy(leaf_hbm.at[k, part], xs.at[k, part], load_sem.at[step, c])

    small = [
        pltpu.make_async_copy(rows_hbm, rows_ref, small_sem.at[0]),
        pltpu.make_async_copy(parent_hbm, parent_ref, small_sem.at[1]),
        pltpu.make_async_copy(map_hbm, map_ref, small_sem.at[2]),
        pltpu.make_async_copy(prow_hbm.at[0], ps, small_sem.at[3]),
    ]
    small[0].start()
    for step in range(2):
        for c in range(pieces):
            load(step, c).start()
    for copy in small[1:]:
        copy.start()

    def direct_copy(u):
        return pltpu.make_async_remote_copy(
            src_ref=gram.at[u, 0],
            dst_ref=direct.at[u],
            send_sem=direct_send.at[u],
            recv_sem=direct_recv.at[u],
            device_id={"row": mod4(r + 2)},
            device_id_type=MESH,
        )

    def far_copy(u, ci, side):
        b0, b1 = CHUNKS[ci]
        return pltpu.make_async_remote_copy(
            src_ref=gram.at[u, b0:b1, pl.ds(64 * side, 64)],
            dst_ref=far.at[u, b0:b1],
            send_sem=far_send.at[u, side, ci],
            recv_sem=far_recv.at[u, ci],
            device_id={"row": mod4(r - 1 + 2 * side)},
            device_id_type=MESH,
        )

    def near_copy(u, ci, side):
        b0, b1 = CHUNKS[ci] if ci >= 0 else (0, 1)
        return pltpu.make_async_remote_copy(
            src_ref=gram.at[u, b0:b1],
            dst_ref=near.at[u, side, b0:b1],
            send_sem=near_send.at[u, ci + 1],
            recv_sem=near_recv.at[u, side, ci + 1],
            device_id={"row": mod4(r - 1 + 2 * side)},
            device_id_type=MESH,
        )

    def start_first(u):
        @pl.when(place[u] == 2)
        def _():
            direct_copy(u).start()
            for side in range(2):
                far_copy(u, 0, side).start()

        for side in range(2):

            @pl.when(place[u] == 1 + 2 * side)
            def _(side=side):
                near_copy(u, -1, side).start()

    def next_far(u, ci):
        @pl.when(place[u] == 2)
        def _():
            for side in range(2):
                far_copy(u, ci, side).start()

    def forward(u, which, waits):
        for side in range(2):

            @pl.when(place[u] == 1 + 2 * side)
            def _(side=side):
                for ci in which:
                    b0, b1 = CHUNKS[ci]
                    far_copy(u, ci, side).wait_recv()
                    half = pl.ds(64 * side, 64)
                    gram[u, b0:b1, half] = gram[u, b0:b1, half] + far[u, b0:b1]
                    if waits and ci:
                        near_copy(u, ci - 2, side).wait_send()
                    near_copy(u, ci, side).start()

    def wait_near(u, ci):
        if ci < 0:
            direct_copy(u).wait_recv()
        for side in range(2):
            near_copy(u, ci, side).wait_recv()

    def drain(u):
        @pl.when(place[u] == 2)
        def _():
            direct_copy(u).wait_send()
            for ci in range(len(CHUNKS)):
                for side in range(2):
                    far_copy(u, ci, side).wait_send()

        for side in range(2):

            @pl.when(place[u] == 1 + 2 * side)
            def _(side=side):
                for ci in (1, 2) if u == 2 else range(-1, 3):
                    near_copy(u, ci, side).wait_send()

    def summed(u, b):
        return gram[u, b] + (near[u, 0, b] + near[u, 1, b])

    def add_gram(x, start):
        high, low = split(x)
        for ref, rows, columns, other in (
            (hh, slice(0, 256), slice(0, N), high),
            (hh, slice(256, N), slice(256, N), high),
            (hl, slice(0, N), slice(0, N), low),
        ):
            value = tn(high[:, rows], other[:, columns])
            ref[rows, columns] = value if start else ref[rows, columns] + value

    def finish_gram(u, scale):
        for b, (i, j) in enumerate(BLOCKS):
            rows, columns = slice(H * i, H * i + H), slice(H * j, H * j + H)
            gram[u, b] = (hh[rows, columns] + (hl[rows, columns] + hl[columns, rows].T)) * scale

    total = 4 * live_rows
    small[0].wait()
    for step in range(2):
        k = first if step == 0 else 1 - first
        live = rows_ref[k] - r * live_rows
        for c in range(pieces):
            load(step, c).wait()
            x = xs[k, pl.ds(c * piece, piece)]
            position = lax.broadcasted_iota(jnp.int32, (piece, N), 0) + c * piece
            add_gram(jnp.where(position < live, x, 0.0), c == 0)
            if step == 1 and c < 2:
                for u in range(2):
                    next_far(u, c + 1)
        finish_gram(k, 1.0 / total)
        if step == 0:
            pl.semaphore_wait(barrier, greeted)
        for u in range(2):

            @pl.when(k == u)
            def _(u=u):
                start_first(u)

    for u in range(2):
        forward(u, (0, 1), False)

    def fill_rows(u, ci):
        wait_near(u, ci)
        add = ci > 0
        b0, b1 = CHUNKS[ci]
        for b in range(b0, b1):
            i, j = BLOCKS[b]
            columns = slice(j * H, j * H + H)
            work[i, :, columns] = work[i, :, columns] + summed(u, b) if add else summed(u, b)

    def factor(u, count, out, beside, after):
        wait_near(u, -1)
        diag[...] = summed(u, 0) + direct[u]
        for b in range(count):
            diagonal, inverse = factor_block(diag[...])
            out[b, b] = diagonal
            beside(b)
            if b < 3:
                if b == 0:
                    fill_rows(u, 0)
                if b == 1:
                    fill_rows(u, 1)
                    fill_rows(u, 2)
                lo = b * H + H
                ih, il = split(inverse)

                def solve(columns):
                    wh, wl = split(work[b, :, columns])
                    return nn(ih, wh) + (nn(ih, wl) + nn(il, wh))

                near_panel = solve(slice(lo, lo + H))
                nh, nl = split(near_panel)
                out[b, b + 1] = near_panel
                diag[...] = work[b + 1, :, lo : lo + H] - tn3(nh, nl, nh, nl)
                if b < 2:
                    rest = solve(slice(lo + H, N))
                    rh, rl = split(rest)
                    for q in range(b + 2, 4):
                        out[b, q] = rest[:, (q - b - 2) * H : (q - b - 1) * H]
                    columns = slice(lo + H, N)
                    taken = tn3(nh, nl, rh, rl)
                    work[b + 1, :, columns] = -taken if b == 0 else work[b + 1, :, columns] - taken
                    for i in range(b + 2, 4):
                        o = (i - b - 2) * H
                        columns = slice(i * H, N)
                        taken = tn3(rh[:, o : o + H], rl[:, o : o + H], rh[:, o:], rl[:, o:])
                        work[i, :, columns] = -taken if b == 0 else work[i, :, columns] - taken
            after(b)

    def lf_copy(k, b, q):
        return pltpu.make_async_remote_copy(
            src_ref=rleaf.at[b, q],
            dst_ref=lf_out.at[k, pl.ds(b * H, H)],
            send_sem=lf_send.at[b, q],
            recv_sem=lf_recv.at[k, b],
            device_id={"row": q},
            device_id_type=MESH,
        )

    def slot_copy(delta):
        return pltpu.make_async_remote_copy(
            src_ref=slots.at[2],
            dst_ref=slots.at[2 + delta],
            send_sem=slot_send.at[2 + delta],
            recv_sem=slot_recv.at[2 + delta],
            device_id={"leaf": l + delta},
            device_id_type=MESH,
        )

    sibling = l + 1 - 2 * core
    onward = 4 * core - 2

    def slot_copy(source, slot, device, send):
        return pltpu.make_async_remote_copy(
            src_ref=slots.at[source],
            dst_ref=slots.at[slot],
            send_sem=slot_send.at[send],
            recv_sem=slot_recv.at[slot],
            device_id={"leaf": device},
            device_id_type=MESH,
        )

    def inside(place_of):
        return jnp.logical_and(place_of >= 0, place_of < leaves)

    def own_slot(delta):
        return slot_copy(2, 2 + delta, l + delta, 2 + delta)

    def sibling_slot():
        return slot_copy(2, 2 + sibling - l, sibling, 1)

    def onward_slot():
        return slot_copy(2 + onward, 1 + 2 * core, sibling, 2)

    @pl.when(factors)
    def _():
        def beside(b):
            if b == 0:
                for u in range(2):
                    forward(u, (2,), False)

        factor(k_here, 2, rleaf, beside, lambda b: None)
        slots[2, 0] = diag[...]
        slots[2, 1] = work[2, :, 384:N]
        slots[2, 2] = work[3, :, 384:N]
        for delta in (-2, 2):

            @pl.when(inside(l + delta))
            def _(delta=delta):
                own_slot(delta).start()

        sibling_slot().start()
    @pl.when(jnp.logical_not(factors))
    def _():
        for u in range(2):
            forward(u, (2,), False)

    for copy in small[1:]:
        copy.wait()
    add_gram(ps[...], True)
    finish_gram(2, 1.0 / (4 * ps.shape[0]))
    for k in range(2):

        @pl.when(r == 0)
        def _(k=k):
            lf_out[k, H : 2 * H] = jnp.zeros((H, H), F32)

    for b in range(1, 4):

        @pl.when(b > r)
        def _(b=b):
            pf_out[0, b * H : b * H + H] = jnp.zeros((H, H), F32)

    @pl.when(factors)
    def _():
        for q in range(4):
            for b in range(min(q, 1) + 1):

                @pl.when(q != r)
                def _(q=q, b=b):
                    lf_copy(k_here, b, q).start()

                @pl.when(q == r)
                def _(q=q, b=b):
                    lf_out[k_here, b * H : b * H + H] = rleaf[b, q]

    def place_slot(i, carry):
        one = 2 * core - 1
        delta = jnp.where(
            factors,
            jnp.where(i == 0, 0, jnp.where(i == 1, onward, -onward)),
            jnp.where(i == 0, one, -one),
        )
        source = l - delta
        valid = jnp.logical_and(jnp.logical_or(factors, i < 2), inside(source))

        @pl.when(valid)
        def _():
            slot = 2 + delta

            @pl.when(delta != 0)
            def _():
                slot_copy(2, slot, sibling, 0).wait_recv()

            @pl.when(jnp.logical_and(factors, i == 1))
            def _():
                onward_slot().start()

            front = 2 * source + lax.rem(r, 2)
            away = jnp.where(parent_ref[front] == l, 0, 2 * N)
            target = map_ref[pl.ds(front, 1), :] + away
            chosen = (lax.broadcasted_iota(jnp.int32, (N, 256), 0) == target).astype(F32).astype(BF16)
            s = slots[slot]
            square = jnp.concatenate(
                [jnp.concatenate([s[0], s[1]], 1), jnp.concatenate([s[1].T, s[2]], 1)], 0
            )
            high, low = split(square)
            high_rows, low_rows = nn(chosen, high).astype(BF16), nn(chosen, low).astype(BF16)
            for half in range(2):
                rows, columns = slice(256 * half, 256 * half + 256), slice(256 * half, N)
                placed = nt(high_rows[rows], chosen[columns]) + nt(low_rows[rows], chosen[columns])
                for b, (bi, bj) in enumerate(BLOCKS):
                    if bi // 2 == half:
                        ii, jj = (bi - 2 * half) * H, (bj - 2 * half) * H
                        gram[2, b] = gram[2, b] + placed[ii : ii + H, jj : jj + H]

        return carry

    lax.fori_loop(0, 3, place_slot, 0)

    start_first(2)
    for ci in (1, 2):
        next_far(2, ci)
    forward(2, (0, 1, 2), True)

    def pf_copy(b, q):
        return pltpu.make_async_remote_copy(
            src_ref=rpar.at[b, q],
            dst_ref=pf_out.at[0, pl.ds(b * H, H)],
            send_sem=pf_send.at[b, q],
            recv_sem=pf_recv.at[b],
            device_id={"row": q},
            device_id_type=MESH,
        )

    @pl.when(place[2] == 0)
    def _():
        def after(b):
            for q in range(b, 4):

                @pl.when(q != r)
                def _(q=q):
                    pf_copy(b, q).start()

                @pl.when(q == r)
                def _(q=q):
                    pf_out[0, b * H : b * H + H] = rpar[b, q]

        factor(2, 4, rpar, lambda b: None, after)
        for q in range(4):

            @pl.when(q != r)
            def _(q=q):
                for b in range(q + 1):
                    pf_copy(b, q).wait_send()

    @pl.when(place[2] != 0)
    def _():
        for b in range(4):

            @pl.when(b <= r)
            def _(b=b):
                pf_copy(b, 0).wait_recv()

    for k in range(2):

        @pl.when(k_mine != k)
        def _(k=k):
            lf_copy(k, 0, 0).wait_recv()

            @pl.when(r > 0)
            def _():
                lf_copy(k, 1, 0).wait_recv()

        @pl.when(k_mine == k)
        def _(k=k):
            for q in range(4):

                @pl.when(q != r)
                def _(q=q):
                    for b in range(min(q, 1) + 1):
                        lf_copy(k, b, q).wait_send()

    @pl.when(factors)
    def _():
        for delta in (-2, 2):

            @pl.when(inside(l + delta))
            def _(delta=delta):
                own_slot(delta).wait_send()

        sibling_slot().wait_send()

        @pl.when(inside(l - onward))
        def _():
            onward_slot().wait_send()

    for u in range(3):
        drain(u)


def hand_over(leaf_in, parent_in, leaf_out, parent_out, leaf_held, parent_held, sems):
    parts = [
        (leaf_in, leaf_held, leaf_out, (k, pl.ds(h * H, H))) for k in range(2) for h in range(2)
    ] + [(parent_in, parent_held, parent_out, (0, pl.ds(h * H, H))) for h in range(4)]
    inward = [
        pltpu.make_async_copy(source.at[part], held.at[part], sems.at[0, i])
        for i, (source, held, target, part) in enumerate(parts)
    ]
    outward = [
        pltpu.make_async_copy(held.at[part], target.at[part], sems.at[1, i])
        for i, (source, held, target, part) in enumerate(parts)
    ]
    for copy in inward:
        copy.start()
    for arrived, copy in zip(inward, outward):
        arrived.wait()
        copy.start()
    for copy in outward:
        copy.wait()


def per_device(leaf_fronts, front_rows, parent_of, column_map, parent_rows):
    kids, live_rows, _ = leaf_fronts.shape
    chunks = len(CHUNKS)
    dma = pltpu.SemaphoreType.DMA
    vmem = pltpu.VMEM
    factors = pl.pallas_call(
        kernel,
        out_shape=(
            jax.ShapeDtypeStruct((kids, 256, H), F32),
            jax.ShapeDtypeStruct((1, N, H), F32),
        ),
        in_specs=[pl.BlockSpec(memory_space=pltpu.HBM)] * 5,
        out_specs=(pl.BlockSpec(memory_space=pltpu.VMEM),) * 2,
        scratch_shapes=[
            pltpu.SMEM(front_rows.shape, jnp.int32),
            pltpu.SMEM(parent_of.shape, jnp.int32),
            vmem(column_map.shape, jnp.int32),
            vmem((kids, live_rows, N), F32),
            vmem(parent_rows.shape[1:], F32),
            vmem((N, N), F32),
            vmem((N, N), F32),
            vmem((3, 10, H, H), F32),
            vmem((3, 10, H // 2, H), F32),
            vmem((3, 2, 10, H, H), F32),
            vmem((3, H, H), F32),
            vmem((4, H, N), F32),
            vmem((H, H), F32),
            vmem((2, 4, H, H), F32),
            vmem((4, 4, H, H), F32),
            vmem((5, 3, H, H), F32),
            dma((2, 2)),
            dma((4,)),
            dma((3,)),
            dma((3,)),
            dma((3, 2, chunks)),
            dma((3, chunks)),
            dma((3, chunks + 1)),
            dma((3, 2, chunks + 1)),
            dma((2, 4)),
            dma((2, 2)),
            dma((5,)),
            dma((5,)),
            dma((4, 4)),
            dma((4,)),
        ],
        compiler_params=pltpu.CompilerParams(
            collective_id=0, has_side_effects=True, vmem_limit_bytes=60 << 20
        ),
        name="fronts",
    )(front_rows, parent_of, column_map, leaf_fronts, parent_rows)
    hbm = pl.BlockSpec(memory_space=pltpu.HBM)
    return pl.pallas_call(
        hand_over,
        out_shape=[jax.ShapeDtypeStruct(x.shape, x.dtype) for x in factors],
        in_specs=[hbm] * 2,
        out_specs=[hbm] * 2,
        scratch_shapes=[vmem(x.shape, x.dtype) for x in factors] + [dma((2, 8))],
        name="hand_over",
    )(*factors)


def solution(mesh):
    return jax.shard_map(
        per_device,
        mesh=mesh,
        in_specs=(P("leaf", "row", None), P("leaf"), P(), P(), P("leaf", "row", None)),
        out_specs=(P("leaf", None, "row"), P("leaf", None, "row")),
        check_vma=False,
    )
```

```python
import jax
import jax.numpy as jnp
from jax import lax
from jax.experimental import pallas as pl
from jax.experimental.pallas import tpu as pltpu
from jax.sharding import PartitionSpec as P

F32, BF16 = jnp.float32, jnp.bfloat16
MESH = pl.DeviceIdType.MESH
N = 512
H = 128
BLOCKS = [(i, j) for i in range(4) for j in range(i, 4)]
CHUNKS = ((1, 5), (5, 7), (7, 10))
REACH = 2


def split(x):
    high = x.astype(BF16)
    return high, (x - high.astype(F32)).astype(BF16)


def nn(a, b):
    return jnp.dot(a, b, preferred_element_type=F32)


def tn(a, b):
    return lax.dot_general(a, b, (((0,), (0,)), ((), ())), preferred_element_type=F32)


def nt(a, b):
    return lax.dot_general(a, b, (((1,), (1,)), ((), ())), preferred_element_type=F32)


def nn3(a, b):
    ah, al = split(a)
    bh, bl = split(b)
    return nn(ah, bh) + (nn(ah, bl) + nn(al, bh))


def nn3_stacked(a, b):
    ah, al = split(a)
    bh, bl = split(b)
    return nn(jnp.concatenate([ah, al, ah], 1), jnp.concatenate([bh, bh, bl], 0))


def tn3(ah, al, bh, bl):
    return tn(ah, bh) + (tn(ah, bl) + tn(al, bh))


def spread_row(x, p):
    return jnp.broadcast_to(x[p : p + 1, :], (8, H))


def spread_column(x, k):
    return jnp.take_along_axis(x, jnp.full((8, H), k, jnp.int32), axis=1)


def tree(terms):
    while len(terms) > 1:
        terms = [terms[i] + terms[i + 1] for i in range(0, len(terms), 2)]
    return terms[0]


def factor_block(a, wanted=2):
    sub = lax.broadcasted_iota(jnp.int32, (8, H), 0)
    lane = lax.broadcasted_iota(jnp.int32, (8, H), 1)
    count = H // 8
    tiles = [
        [a[8 * t : 8 * t + 8, :], (lane == sub + 8 * t).astype(F32)][:wanted] for t in range(count)
    ]
    results = []
    for t in range(count):
        j = 8 * t
        now = tiles[t]
        column = [spread_column(now[0], j + k) for k in range(8)]
        if t + 1 < count:
            following = [spread_column(tiles[t + 1][0], j + k) for k in range(8)]
        rows = [jnp.zeros((8, H), F32) for _ in now]
        for p in range(8):
            here = sub == p
            pivot = spread_row(column[p], p)
            inv = 1.0 / pivot
            root = lax.rsqrt(pivot)
            signed = jnp.where(here, -1.0, column[p])

            def eliminate(z):
                return jnp.where(here, 0.0, z) - (signed * spread_row(z, p)) * inv

            rows = [jnp.where(here, x * root, kept) for x, kept in zip(now, rows)]
            for k in range(p + 1, 8):
                column[k] = eliminate(column[k])
            now = [eliminate(x) for x in now]
        results.append([jnp.where(lane >= sub + j, rows[0], 0.0)] + rows[1:])
        if t + 1 < count:
            nxt = [
                old - tree([following[p] * spread_row(new, p) for p in range(8)])
                for old, new in zip(tiles[t + 1], now)
            ]
            if t + 2 < count:
                below = jnp.concatenate([tiles[u][0] for u in range(t + 2, count)], 0)
                parts = [jnp.concatenate(now, 1)] if wanted > 1 else list(now)
                if j:
                    parts = [jnp.zeros((j, wanted * H), F32)] + parts
                parts.append(jnp.zeros((H - 8 - j, wanted * H), F32))
                change = nn3_stacked(below, jnp.concatenate(parts, 0))
                for u in range(t + 2, count):
                    taken = change[8 * (u - t - 2) : 8 * (u - t - 1)]
                    tiles[u] = [x - taken[:, i * H : i * H + H] for i, x in enumerate(tiles[u])]
            tiles[t + 1] = nxt
    return [jnp.concatenate(x, 0) for x in zip(*results)]


def kernel(
    rows_hbm, parent_hbm, map_hbm, leaf_hbm, prow_hbm, lf_out, pf_out,
    rows_ref, parent_ref, map_ref, xs, ps, hh, hl, gram, far, near, direct,
    work, diag, rleaf, rpar, slots,
    load_sem, small_sem, direct_send, direct_recv, far_send, far_recv, near_send, near_recv,
    lf_send, lf_recv, slot_send, slot_recv, pf_send, pf_recv,
):
    r = lax.axis_index("row")
    l = lax.axis_index("leaf")
    leaves = lax.axis_size("leaf")
    core = lax.rem(l, 2)
    live_rows = xs.shape[1]
    pieces = load_sem.shape[1]
    piece = live_rows // pieces

    def mod4(v):
        return lax.rem(v + 8, 4)

    base = 2 - 2 * core
    place = [mod4(r - (base + k)) for k in range(2)]
    first = jnp.where(jnp.logical_or(place[0] == 0, place[0] == 3), 1, 0)
    rp = 3 - core
    place.append(mod4(r - rp))
    k_mine = r - base
    factors = jnp.logical_and(k_mine >= 0, k_mine < 2)
    k_here = jnp.clip(k_mine, 0, 1)

    barrier = pltpu.get_barrier_semaphore()
    for step in (1, 2, 3):
        pl.semaphore_signal(barrier, inc=1, device_id={"row": mod4(r + step)}, device_id_type=MESH)
    greeted = 3
    for delta in (-2, -1, 1, 2):
        there = jnp.logical_and(l + delta >= 0, l + delta < leaves)

        @pl.when(there)
        def _(delta=delta):
            pl.semaphore_signal(barrier, inc=1, device_id={"leaf": l + delta}, device_id_type=MESH)

        greeted = greeted + jnp.where(there, 1, 0)

    def load(step, c):
        k = first if step == 0 else 1 - first
        part = pl.ds(c * piece, piece)
        return pltpu.make_async_copy(leaf_hbm.at[k, part], xs.at[k, part], load_sem.at[step, c])

    small = [
        pltpu.make_async_copy(rows_hbm, rows_ref, small_sem.at[0]),
        pltpu.make_async_copy(parent_hbm, parent_ref, small_sem.at[1]),
        pltpu.make_async_copy(map_hbm, map_ref, small_sem.at[2]),
        pltpu.make_async_copy(prow_hbm.at[0], ps, small_sem.at[3]),
    ]
    small[0].start()
    for step in range(2):
        for c in range(pieces):
            load(step, c).start()
    for copy in small[1:]:
        copy.start()

    def direct_copy(u):
        return pltpu.make_async_remote_copy(
            src_ref=gram.at[u, 0],
            dst_ref=direct.at[u],
            send_sem=direct_send.at[u],
            recv_sem=direct_recv.at[u],
            device_id={"row": mod4(r + 2)},
            device_id_type=MESH,
        )

    def far_copy(u, ci, side):
        b0, b1 = CHUNKS[ci]
        return pltpu.make_async_remote_copy(
            src_ref=gram.at[u, b0:b1, pl.ds(64 * side, 64)],
            dst_ref=far.at[u, b0:b1],
            send_sem=far_send.at[u, side, ci],
            recv_sem=far_recv.at[u, ci],
            device_id={"row": mod4(r - 1 + 2 * side)},
            device_id_type=MESH,
        )

    def near_copy(u, ci, side):
        b0, b1 = CHUNKS[ci] if ci >= 0 else (0, 1)
        return pltpu.make_async_remote_copy(
            src_ref=gram.at[u, b0:b1],
            dst_ref=near.at[u, side, b0:b1],
            send_sem=near_send.at[u, ci + 1],
            recv_sem=near_recv.at[u, side, ci + 1],
            device_id={"row": mod4(r - 1 + 2 * side)},
            device_id_type=MESH,
        )

    def start_first(u):
        @pl.when(place[u] == 2)
        def _():
            direct_copy(u).start()

        for side in range(2):

            @pl.when(place[u] == 1 + 2 * side)
            def _(side=side):
                near_copy(u, -1, side).start()

    def next_far(u, ci):
        @pl.when(place[u] == 2)
        def _():
            for side in range(2):
                far_copy(u, ci, side).start()

    def forward(u, which, waits):
        for side in range(2):

            @pl.when(place[u] == 1 + 2 * side)
            def _(side=side):
                for ci in which:
                    b0, b1 = CHUNKS[ci]
                    far_copy(u, ci, side).wait_recv()
                    half = pl.ds(64 * side, 64)
                    gram[u, b0:b1, half] = gram[u, b0:b1, half] + far[u, b0:b1]
                    if waits and ci:
                        near_copy(u, ci - 2, side).wait_send()
                    near_copy(u, ci, side).start()

    def wait_near(u, ci):
        if ci < 0:
            direct_copy(u).wait_recv()
        for side in range(2):
            near_copy(u, ci, side).wait_recv()

    def drain(u):
        @pl.when(place[u] == 2)
        def _():
            direct_copy(u).wait_send()
            for ci in range(len(CHUNKS)):
                for side in range(2):
                    far_copy(u, ci, side).wait_send()

        for side in range(2):

            @pl.when(place[u] == 1 + 2 * side)
            def _(side=side):
                for ci in (1, 2) if u == 2 else range(-1, 3):
                    near_copy(u, ci, side).wait_send()

    def summed(u, b):
        return gram[u, b] + (near[u, 0, b] + near[u, 1, b])

    def add_gram(x, start):
        high, low = split(x)
        for ref, rows, columns, other in (
            (hh, slice(0, 256), slice(0, N), high),
            (hh, slice(256, N), slice(256, N), high),
            (hl, slice(0, N), slice(0, N), low),
        ):
            value = tn(high[:, rows], other[:, columns])
            ref[rows, columns] = value if start else ref[rows, columns] + value

    def finish_gram(u, scale, b0, b1):
        for b in range(b0, b1):
            i, j = BLOCKS[b]
            rows, columns = slice(H * i, H * i + H), slice(H * j, H * j + H)
            gram[u, b] = (hh[rows, columns] + (hl[rows, columns] + hl[columns, rows].T)) * scale

    total = 4 * live_rows
    small[0].wait()
    for step in range(2):
        k = first if step == 0 else 1 - first
        live = rows_ref[k] - r * live_rows
        for c in range(pieces):
            load(step, c).wait()
            x = xs[k, pl.ds(c * piece, piece)]
            position = lax.broadcasted_iota(jnp.int32, (piece, N), 0) + c * piece
            add_gram(jnp.where(position < live, x, 0.0), c == 0)
            if step == 1 and c < 2:
                for u in range(2):
                    next_far(u, c + 1)
        finish_gram(k, 1.0 / total, 0, 1)
        if step == 0:
            pl.semaphore_wait(barrier, greeted)
        for u in range(2):

            @pl.when(k == u)
            def _(u=u):
                start_first(u)

        finish_gram(k, 1.0 / total, 1, 10)
        if step == 0:
            for u in range(2):
                next_far(u, 0)

    for u in range(2):
        forward(u, (0,), False)

    def fill_rows(u, ci):
        wait_near(u, ci)
        add = ci > 0
        b0, b1 = CHUNKS[ci]
        for b in range(b0, b1):
            i, j = BLOCKS[b]
            columns = slice(j * H, j * H + H)
            work[i, :, columns] = work[i, :, columns] + summed(u, b) if add else summed(u, b)

    def factor(u, count, out, beside, after):
        wait_near(u, -1)
        diag[...] = summed(u, 0) + direct[u]
        for b in range(count):
            diagonal, *inverse = factor_block(diag[...], 1 if b == 3 else 2)
            out[b, b] = diagonal
            beside(b)
            if b < 3:
                if b == 0:
                    fill_rows(u, 0)
                if b == 1:
                    fill_rows(u, 1)
                    fill_rows(u, 2)
                lo = b * H + H
                ih, il = split(inverse[0])

                def solve(columns):
                    wh, wl = split(work[b, :, columns])
                    return nn(ih, wh) + (nn(ih, wl) + nn(il, wh))

                near_panel = solve(slice(lo, lo + H))
                nh, nl = split(near_panel)
                out[b, b + 1] = near_panel
                diag[...] = work[b + 1, :, lo : lo + H] - tn3(nh, nl, nh, nl)
                if b < 2:
                    rest = solve(slice(lo + H, N))
                    rh, rl = split(rest)
                    for q in range(b + 2, 4):
                        out[b, q] = rest[:, (q - b - 2) * H : (q - b - 1) * H]
                    columns = slice(lo + H, N)
                    taken = tn3(nh, nl, rh, rl)
                    work[b + 1, :, columns] = -taken if b == 0 else work[b + 1, :, columns] - taken
                    for i in range(b + 2, 4):
                        o = (i - b - 2) * H
                        columns = slice(i * H, N)
                        taken = tn3(rh[:, o : o + H], rl[:, o : o + H], rh[:, o:], rl[:, o:])
                        work[i, :, columns] = -taken if b == 0 else work[i, :, columns] - taken
            after(b)

    def lf_copy(k, b, q):
        return pltpu.make_async_remote_copy(
            src_ref=rleaf.at[b, q],
            dst_ref=lf_out.at[k, pl.ds(b * H, H)],
            send_sem=lf_send.at[b, q],
            recv_sem=lf_recv.at[k, b],
            device_id={"row": q},
            device_id_type=MESH,
        )

    def slot_copy(delta):
        return pltpu.make_async_remote_copy(
            src_ref=slots.at[2],
            dst_ref=slots.at[2 + delta],
            send_sem=slot_send.at[2 + delta],
            recv_sem=slot_recv.at[2 + delta],
            device_id={"leaf": l + delta},
            device_id_type=MESH,
        )

    sibling = l + 1 - 2 * core
    onward = 4 * core - 2

    def slot_copy(source, slot, device, send):
        return pltpu.make_async_remote_copy(
            src_ref=slots.at[source],
            dst_ref=slots.at[slot],
            send_sem=slot_send.at[send],
            recv_sem=slot_recv.at[slot],
            device_id={"leaf": device},
            device_id_type=MESH,
        )

    def inside(place_of):
        return jnp.logical_and(place_of >= 0, place_of < leaves)

    def own_slot(delta):
        return slot_copy(2, 2 + delta, l + delta, 2 + delta)

    def sibling_slot():
        return slot_copy(2, 2 + sibling - l, sibling, 1)

    def onward_slot():
        return slot_copy(2 + onward, 1 + 2 * core, sibling, 2)

    @pl.when(factors)
    def _():
        def beside(b):
            if b == 0:
                for u in range(2):
                    forward(u, (1, 2), False)

        factor(k_here, 2, rleaf, beside, lambda b: None)
        slots[2, 0] = diag[...]
        slots[2, 1] = work[2, :, 384:N]
        slots[2, 2] = work[3, :, 384:N]
        for delta in (-2, 2):

            @pl.when(inside(l + delta))
            def _(delta=delta):
                own_slot(delta).start()

        sibling_slot().start()
    @pl.when(jnp.logical_not(factors))
    def _():
        for u in range(2):
            forward(u, (1, 2), False)

    for copy in small[1:]:
        copy.wait()
    add_gram(ps[...], True)
    finish_gram(2, 1.0 / (4 * ps.shape[0]), 0, 10)
    for k in range(2):

        @pl.when(r == 0)
        def _(k=k):
            lf_out[k, H : 2 * H] = jnp.zeros((H, H), F32)

    for b in range(1, 4):

        @pl.when(b > r)
        def _(b=b):
            pf_out[0, b * H : b * H + H] = jnp.zeros((H, H), F32)

    @pl.when(factors)
    def _():
        for q in range(4):
            for b in range(min(q, 1) + 1):

                @pl.when(q != r)
                def _(q=q, b=b):
                    lf_copy(k_here, b, q).start()

                @pl.when(q == r)
                def _(q=q, b=b):
                    lf_out[k_here, b * H : b * H + H] = rleaf[b, q]

    def place_slot(i, carry):
        one = 2 * core - 1
        delta = jnp.where(
            factors,
            jnp.where(i == 0, 0, jnp.where(i == 1, onward, -onward)),
            jnp.where(i == 0, one, -one),
        )
        source = l - delta
        valid = jnp.logical_and(jnp.logical_or(factors, i < 2), inside(source))

        @pl.when(valid)
        def _():
            slot = 2 + delta

            @pl.when(delta != 0)
            def _():
                slot_copy(2, slot, sibling, 0).wait_recv()

            @pl.when(jnp.logical_and(factors, i == 1))
            def _():
                onward_slot().start()

            front = 2 * source + lax.rem(r, 2)
            away = jnp.where(parent_ref[front] == l, 0, 2 * N)
            target = map_ref[pl.ds(front, 1), :] + away
            chosen = (lax.broadcasted_iota(jnp.int32, (N, 256), 0) == target).astype(F32).astype(BF16)
            s = slots[slot]
            square = jnp.concatenate(
                [jnp.concatenate([s[0], s[1]], 1), jnp.concatenate([s[1].T, s[2]], 1)], 0
            )
            high, low = split(square)
            high_rows, low_rows = nn(chosen, high).astype(BF16), nn(chosen, low).astype(BF16)
            for half in range(2):
                rows, columns = slice(256 * half, 256 * half + 256), slice(256 * half, N)
                placed = nt(high_rows[rows], chosen[columns]) + nt(low_rows[rows], chosen[columns])
                for b, (bi, bj) in enumerate(BLOCKS):
                    if bi // 2 == half:
                        ii, jj = (bi - 2 * half) * H, (bj - 2 * half) * H
                        gram[2, b] = gram[2, b] + placed[ii : ii + H, jj : jj + H]

        return carry

    lax.fori_loop(0, 3, place_slot, 0)

    start_first(2)
    for ci in (0, 1, 2):
        next_far(2, ci)
    forward(2, (0, 1, 2), True)

    def pf_copy(b, q):
        return pltpu.make_async_remote_copy(
            src_ref=rpar.at[b, q],
            dst_ref=pf_out.at[0, pl.ds(b * H, H)],
            send_sem=pf_send.at[b, q],
            recv_sem=pf_recv.at[b],
            device_id={"row": q},
            device_id_type=MESH,
        )

    @pl.when(place[2] == 0)
    def _():
        def after(b):
            for q in range(b, 4):

                @pl.when(q != r)
                def _(q=q):
                    pf_copy(b, q).start()

                @pl.when(q == r)
                def _(q=q):
                    pf_out[0, b * H : b * H + H] = rpar[b, q]

        factor(2, 4, rpar, lambda b: None, after)
        for q in range(4):

            @pl.when(q != r)
            def _(q=q):
                for b in range(q + 1):
                    pf_copy(b, q).wait_send()

    @pl.when(place[2] != 0)
    def _():
        for b in range(4):

            @pl.when(b <= r)
            def _(b=b):
                pf_copy(b, 0).wait_recv()

    for k in range(2):

        @pl.when(k_mine != k)
        def _(k=k):
            lf_copy(k, 0, 0).wait_recv()

            @pl.when(r > 0)
            def _():
                lf_copy(k, 1, 0).wait_recv()

        @pl.when(k_mine == k)
        def _(k=k):
            for q in range(4):

                @pl.when(q != r)
                def _(q=q):
                    for b in range(min(q, 1) + 1):
                        lf_copy(k, b, q).wait_send()

    @pl.when(factors)
    def _():
        for delta in (-2, 2):

            @pl.when(inside(l + delta))
            def _(delta=delta):
                own_slot(delta).wait_send()

        sibling_slot().wait_send()

        @pl.when(inside(l - onward))
        def _():
            onward_slot().wait_send()

    for u in range(3):
        drain(u)


def hand_over(leaf_in, parent_in, leaf_out, parent_out, leaf_held, parent_held, sems):
    parts = [
        (leaf_in, leaf_held, leaf_out, (k, pl.ds(h * H, H))) for k in range(2) for h in range(2)
    ] + [(parent_in, parent_held, parent_out, (0, pl.ds(h * H, H))) for h in range(4)]
    inward = [
        pltpu.make_async_copy(source.at[part], held.at[part], sems.at[0, i])
        for i, (source, held, target, part) in enumerate(parts)
    ]
    outward = [
        pltpu.make_async_copy(held.at[part], target.at[part], sems.at[1, i])
        for i, (source, held, target, part) in enumerate(parts)
    ]
    for copy in inward:
        copy.start()
    for arrived, copy in zip(inward, outward):
        arrived.wait()
        copy.start()
    for copy in outward:
        copy.wait()


def per_device(leaf_fronts, front_rows, parent_of, column_map, parent_rows):
    kids, live_rows, _ = leaf_fronts.shape
    chunks = len(CHUNKS)
    dma = pltpu.SemaphoreType.DMA
    vmem = pltpu.VMEM
    factors = pl.pallas_call(
        kernel,
        out_shape=(
            jax.ShapeDtypeStruct((kids, 256, H), F32),
            jax.ShapeDtypeStruct((1, N, H), F32),
        ),
        in_specs=[pl.BlockSpec(memory_space=pltpu.HBM)] * 5,
        out_specs=(pl.BlockSpec(memory_space=pltpu.VMEM),) * 2,
        scratch_shapes=[
            pltpu.SMEM(front_rows.shape, jnp.int32),
            pltpu.SMEM(parent_of.shape, jnp.int32),
            vmem(column_map.shape, jnp.int32),
            vmem((kids, live_rows, N), F32),
            vmem(parent_rows.shape[1:], F32),
            vmem((N, N), F32),
            vmem((N, N), F32),
            vmem((3, 10, H, H), F32),
            vmem((3, 10, H // 2, H), F32),
            vmem((3, 2, 10, H, H), F32),
            vmem((3, H, H), F32),
            vmem((4, H, N), F32),
            vmem((H, H), F32),
            vmem((2, 4, H, H), F32),
            vmem((4, 4, H, H), F32),
            vmem((5, 3, H, H), F32),
            dma((2, 2)),
            dma((4,)),
            dma((3,)),
            dma((3,)),
            dma((3, 2, chunks)),
            dma((3, chunks)),
            dma((3, chunks + 1)),
            dma((3, 2, chunks + 1)),
            dma((2, 4)),
            dma((2, 2)),
            dma((5,)),
            dma((5,)),
            dma((4, 4)),
            dma((4,)),
        ],
        compiler_params=pltpu.CompilerParams(
            collective_id=0, has_side_effects=True, vmem_limit_bytes=60 << 20
        ),
        name="fronts",
    )(front_rows, parent_of, column_map, leaf_fronts, parent_rows)
    hbm = pl.BlockSpec(memory_space=pltpu.HBM)
    return pl.pallas_call(
        hand_over,
        out_shape=[jax.ShapeDtypeStruct(x.shape, x.dtype) for x in factors],
        in_specs=[hbm] * 2,
        out_specs=[hbm] * 2,
        scratch_shapes=[vmem(x.shape, x.dtype) for x in factors] + [dma((2, 8))],
        name="hand_over",
    )(*factors)


def solution(mesh):
    return jax.shard_map(
        per_device,
        mesh=mesh,
        in_specs=(P("leaf", "row", None), P("leaf"), P(), P(), P("leaf", "row", None)),
        out_specs=(P("leaf", None, "row"), P("leaf", None, "row")),
        check_vma=False,
    )
```

```python
import jax
import jax.numpy as jnp
from jax import lax
from jax.experimental import pallas as pl
from jax.experimental.pallas import tpu as pltpu
from jax.sharding import PartitionSpec as P

F32, BF16 = jnp.float32, jnp.bfloat16
MESH = pl.DeviceIdType.MESH
N = 512
H = 128
BLOCKS = [(i, j) for i in range(4) for j in range(i, 4)]
CHUNKS = ((1, 5), (5, 7), (7, 10))
REACH = 2


def split(x):
    high = x.astype(BF16)
    return high, (x - high.astype(F32)).astype(BF16)


def nn(a, b):
    return jnp.dot(a, b, preferred_element_type=F32)


def tn(a, b):
    return lax.dot_general(a, b, (((0,), (0,)), ((), ())), preferred_element_type=F32)


def nt(a, b):
    return lax.dot_general(a, b, (((1,), (1,)), ((), ())), preferred_element_type=F32)


def nn3(a, b):
    ah, al = split(a)
    bh, bl = split(b)
    return nn(ah, bh) + (nn(ah, bl) + nn(al, bh))


def nn3_stacked(a, b):
    ah, al = split(a)
    bh, bl = split(b)
    return nn(jnp.concatenate([ah, al, ah], 1), jnp.concatenate([bh, bh, bl], 0))


def tn3(ah, al, bh, bl):
    return tn(ah, bh) + (tn(ah, bl) + tn(al, bh))


def spread_row(x, p):
    return jnp.broadcast_to(x[p : p + 1, :], (8, H))


def spread_column(x, k):
    return jnp.take_along_axis(x, jnp.full((8, H), k, jnp.int32), axis=1)


def tree(terms):
    while len(terms) > 1:
        terms = [terms[i] + terms[i + 1] for i in range(0, len(terms), 2)]
    return terms[0]


def factor_block(a, wanted=2):
    sub = lax.broadcasted_iota(jnp.int32, (8, H), 0)
    lane = lax.broadcasted_iota(jnp.int32, (8, H), 1)
    count = H // 8
    tiles = [
        [a[8 * t : 8 * t + 8, :], (lane == sub + 8 * t).astype(F32)][:wanted] for t in range(count)
    ]
    results = []
    for t in range(count):
        j = 8 * t
        now = tiles[t]
        column = [spread_column(now[0], j + k) for k in range(8)]
        if t + 1 < count:
            following = [spread_column(tiles[t + 1][0], j + k) for k in range(8)]
        rows = [jnp.zeros((8, H), F32) for _ in now]
        for p in range(8):
            here = sub == p
            pivot = spread_row(column[p], p)
            inv = 1.0 / pivot
            root = lax.rsqrt(pivot)
            signed = jnp.where(here, -1.0, column[p])

            def eliminate(z):
                return jnp.where(here, 0.0, z) - (signed * spread_row(z, p)) * inv

            rows = [jnp.where(here, x * root, kept) for x, kept in zip(now, rows)]
            for k in range(p + 1, 8):
                column[k] = eliminate(column[k])
            now = [eliminate(x) for x in now]
        results.append([jnp.where(lane >= sub + j, rows[0], 0.0)] + rows[1:])
        if t + 1 < count:
            nxt = [
                old - tree([following[p] * spread_row(new, p) for p in range(8)])
                for old, new in zip(tiles[t + 1], now)
            ]
            if t + 2 < count:
                below = jnp.concatenate([tiles[u][0] for u in range(t + 2, count)], 0)
                parts = [jnp.concatenate(now, 1)] if wanted > 1 else list(now)
                if j:
                    parts = [jnp.zeros((j, wanted * H), F32)] + parts
                parts.append(jnp.zeros((H - 8 - j, wanted * H), F32))
                change = nn3_stacked(below, jnp.concatenate(parts, 0))
                for u in range(t + 2, count):
                    taken = change[8 * (u - t - 2) : 8 * (u - t - 1)]
                    tiles[u] = [x - taken[:, i * H : i * H + H] for i, x in enumerate(tiles[u])]
            tiles[t + 1] = nxt
    return [jnp.concatenate(x, 0) for x in zip(*results)]


def kernel(
    rows_hbm, parent_hbm, map_hbm, leaf_hbm, prow_hbm, lf_out, pf_out,
    rows_ref, parent_ref, map_ref, xs, ps, hh, hl, gram, far, near, direct,
    work, diag, rleaf, rpar, slots,
    load_sem, small_sem, direct_send, direct_recv, far_send, far_recv, near_send, near_recv,
    lf_send, lf_recv, slot_send, slot_recv, pf_send, pf_recv,
):
    r = lax.axis_index("row")
    l = lax.axis_index("leaf")
    leaves = lax.axis_size("leaf")
    core = lax.rem(l, 2)
    live_rows = xs.shape[1]
    pieces = load_sem.shape[1]
    piece = live_rows // pieces

    def mod4(v):
        return lax.rem(v + 8, 4)

    base = 2 - 2 * core
    place = [mod4(r - (base + k)) for k in range(2)]
    first = jnp.where(jnp.logical_or(place[0] == 0, place[0] == 3), 1, 0)
    rp = 3 - core
    place.append(mod4(r - rp))
    k_mine = r - base
    factors = jnp.logical_and(k_mine >= 0, k_mine < 2)
    k_here = jnp.clip(k_mine, 0, 1)

    barrier = pltpu.get_barrier_semaphore()
    for step in (1, 2, 3):
        pl.semaphore_signal(barrier, inc=1, device_id={"row": mod4(r + step)}, device_id_type=MESH)
    greeted = 3
    for delta in (-2, -1, 1, 2):
        there = jnp.logical_and(l + delta >= 0, l + delta < leaves)

        @pl.when(there)
        def _(delta=delta):
            pl.semaphore_signal(barrier, inc=1, device_id={"leaf": l + delta}, device_id_type=MESH)

        greeted = greeted + jnp.where(there, 1, 0)

    def load(step, c):
        k = first if step == 0 else 1 - first
        part = pl.ds(c * piece, piece)
        return pltpu.make_async_copy(leaf_hbm.at[k, part], xs.at[k, part], load_sem.at[step, c])

    small = [
        pltpu.make_async_copy(rows_hbm, rows_ref, small_sem.at[0]),
        pltpu.make_async_copy(parent_hbm, parent_ref, small_sem.at[1]),
        pltpu.make_async_copy(map_hbm, map_ref, small_sem.at[2]),
        pltpu.make_async_copy(prow_hbm.at[0], ps, small_sem.at[3]),
    ]
    small[0].start()
    for step in range(2):
        for c in range(pieces):
            load(step, c).start()
    for copy in small[1:]:
        copy.start()

    def direct_copy(u):
        return pltpu.make_async_remote_copy(
            src_ref=gram.at[u, 0],
            dst_ref=direct.at[u],
            send_sem=direct_send.at[u],
            recv_sem=direct_recv.at[u],
            device_id={"row": mod4(r + 2)},
            device_id_type=MESH,
        )

    def far_copy(u, ci, side):
        b0, b1 = CHUNKS[ci]
        return pltpu.make_async_remote_copy(
            src_ref=gram.at[u, b0:b1, pl.ds(64 * side, 64)],
            dst_ref=far.at[u, b0:b1],
            send_sem=far_send.at[u, side, ci],
            recv_sem=far_recv.at[u, ci],
            device_id={"row": mod4(r - 1 + 2 * side)},
            device_id_type=MESH,
        )

    def near_copy(u, ci, side):
        b0, b1 = CHUNKS[ci] if ci >= 0 else (0, 1)
        return pltpu.make_async_remote_copy(
            src_ref=gram.at[u, b0:b1],
            dst_ref=near.at[u, side, b0:b1],
            send_sem=near_send.at[u, ci + 1],
            recv_sem=near_recv.at[u, side, ci + 1],
            device_id={"row": mod4(r - 1 + 2 * side)},
            device_id_type=MESH,
        )

    def start_first(u):
        @pl.when(place[u] == 2)
        def _():
            direct_copy(u).start()

        for side in range(2):

            @pl.when(place[u] == 1 + 2 * side)
            def _(side=side):
                near_copy(u, -1, side).start()

    def next_far(u, ci):
        @pl.when(place[u] == 2)
        def _():
            for side in range(2):
                far_copy(u, ci, side).start()

    def forward(u, which, waits):
        for side in range(2):

            @pl.when(place[u] == 1 + 2 * side)
            def _(side=side):
                for ci in which:
                    b0, b1 = CHUNKS[ci]
                    far_copy(u, ci, side).wait_recv()
                    half = pl.ds(64 * side, 64)
                    gram[u, b0:b1, half] = gram[u, b0:b1, half] + far[u, b0:b1]
                    if waits and ci:
                        near_copy(u, ci - 2, side).wait_send()
                    near_copy(u, ci, side).start()

    def wait_near(u, ci):
        if ci < 0:
            direct_copy(u).wait_recv()
        for side in range(2):
            near_copy(u, ci, side).wait_recv()

    def drain(u):
        @pl.when(place[u] == 2)
        def _():
            direct_copy(u).wait_send()
            for ci in range(len(CHUNKS)):
                for side in range(2):
                    far_copy(u, ci, side).wait_send()

        for side in range(2):

            @pl.when(place[u] == 1 + 2 * side)
            def _(side=side):
                for ci in (1, 2) if u == 2 else range(-1, 3):
                    near_copy(u, ci, side).wait_send()

    def summed(u, b):
        return gram[u, b] + (near[u, 0, b] + near[u, 1, b])

    def add_gram(x, start):
        high, low = split(x)
        for ref, rows, columns, other in (
            (hh, slice(0, 256), slice(0, N), high),
            (hh, slice(256, N), slice(256, N), high),
            (hl, slice(0, N), slice(0, N), low),
        ):
            value = tn(high[:, rows], other[:, columns])
            ref[rows, columns] = value if start else ref[rows, columns] + value

    def finish_gram(u, scale, b0, b1):
        for b in range(b0, b1):
            i, j = BLOCKS[b]
            rows, columns = slice(H * i, H * i + H), slice(H * j, H * j + H)
            gram[u, b] = (hh[rows, columns] + (hl[rows, columns] + hl[columns, rows].T)) * scale

    total = 4 * live_rows
    small[0].wait()
    for step in range(2):
        k = first if step == 0 else 1 - first
        live = rows_ref[k] - r * live_rows
        for c in range(pieces):
            load(step, c).wait()
            x = xs[k, pl.ds(c * piece, piece)]
            position = lax.broadcasted_iota(jnp.int32, (piece, N), 0) + c * piece
            add_gram(jnp.where(position < live, x, 0.0), c == 0)
            if step == 1 and c < 2:
                for u in range(2):
                    next_far(u, c + 1)
        finish_gram(k, 1.0 / total, 0, 1)
        if step == 0:
            pl.semaphore_wait(barrier, greeted)
        for u in range(2):

            @pl.when(k == u)
            def _(u=u):
                start_first(u)

        finish_gram(k, 1.0 / total, 1, 10)
        if step == 0:
            for u in range(2):
                next_far(u, 0)

    for u in range(2):
        forward(u, (0, 1), False)

    def fill_rows(u, ci):
        wait_near(u, ci)
        add = ci > 0
        b0, b1 = CHUNKS[ci]
        for b in range(b0, b1):
            i, j = BLOCKS[b]
            columns = slice(j * H, j * H + H)
            work[i, :, columns] = work[i, :, columns] + summed(u, b) if add else summed(u, b)

    def factor(u, count, out, beside, after):
        wait_near(u, -1)
        diag[...] = summed(u, 0) + direct[u]
        for b in range(count):
            diagonal, *inverse = factor_block(diag[...], 1 if b == 3 else 2)
            out[b, b] = diagonal
            beside(b)
            if b < 3:
                if b == 0:
                    fill_rows(u, 0)
                if b == 1:
                    fill_rows(u, 1)
                    fill_rows(u, 2)
                lo = b * H + H
                ih, il = split(inverse[0])

                def solve(columns):
                    wh, wl = split(work[b, :, columns])
                    return nn(ih, wh) + (nn(ih, wl) + nn(il, wh))

                near_panel = solve(slice(lo, lo + H))
                nh, nl = split(near_panel)
                out[b, b + 1] = near_panel
                diag[...] = work[b + 1, :, lo : lo + H] - tn3(nh, nl, nh, nl)
                if b < 2:
                    rest = solve(slice(lo + H, N))
                    rh, rl = split(rest)
                    for q in range(b + 2, 4):
                        out[b, q] = rest[:, (q - b - 2) * H : (q - b - 1) * H]
                    columns = slice(lo + H, N)
                    taken = tn3(nh, nl, rh, rl)
                    work[b + 1, :, columns] = -taken if b == 0 else work[b + 1, :, columns] - taken
                    for i in range(b + 2, 4):
                        o = (i - b - 2) * H
                        columns = slice(i * H, N)
                        taken = tn3(rh[:, o : o + H], rl[:, o : o + H], rh[:, o:], rl[:, o:])
                        work[i, :, columns] = -taken if b == 0 else work[i, :, columns] - taken
            after(b)

    def lf_copy(k, b, q):
        return pltpu.make_async_remote_copy(
            src_ref=rleaf.at[b, q],
            dst_ref=lf_out.at[k, pl.ds(b * H, H)],
            send_sem=lf_send.at[b, q],
            recv_sem=lf_recv.at[k, b],
            device_id={"row": q},
            device_id_type=MESH,
        )

    def slot_copy(delta):
        return pltpu.make_async_remote_copy(
            src_ref=slots.at[2],
            dst_ref=slots.at[2 + delta],
            send_sem=slot_send.at[2 + delta],
            recv_sem=slot_recv.at[2 + delta],
            device_id={"leaf": l + delta},
            device_id_type=MESH,
        )

    sibling = l + 1 - 2 * core
    onward = 4 * core - 2

    def slot_copy(source, slot, device, send):
        return pltpu.make_async_remote_copy(
            src_ref=slots.at[source],
            dst_ref=slots.at[slot],
            send_sem=slot_send.at[send],
            recv_sem=slot_recv.at[slot],
            device_id={"leaf": device},
            device_id_type=MESH,
        )

    def inside(place_of):
        return jnp.logical_and(place_of >= 0, place_of < leaves)

    def own_slot(delta):
        return slot_copy(2, 2 + delta, l + delta, 2 + delta)

    def sibling_slot():
        return slot_copy(2, 2 + sibling - l, sibling, 1)

    def onward_slot():
        return slot_copy(2 + onward, 1 + 2 * core, sibling, 2)

    @pl.when(factors)
    def _():
        def beside(b):
            if b == 0:
                for u in range(2):
                    forward(u, (2,), False)

        factor(k_here, 2, rleaf, beside, lambda b: None)
        slots[2, 0] = diag[...]
        slots[2, 1] = work[2, :, 384:N]
        slots[2, 2] = work[3, :, 384:N]
        for delta in (-2, 2):

            @pl.when(inside(l + delta))
            def _(delta=delta):
                own_slot(delta).start()

        sibling_slot().start()
    @pl.when(jnp.logical_not(factors))
    def _():
        for u in range(2):
            forward(u, (2,), False)

    for copy in small[1:]:
        copy.wait()
    add_gram(ps[...], True)
    finish_gram(2, 1.0 / (4 * ps.shape[0]), 0, 10)
    for k in range(2):

        @pl.when(r == 0)
        def _(k=k):
            lf_out[k, H : 2 * H] = jnp.zeros((H, H), F32)

    for b in range(1, 4):

        @pl.when(b > r)
        def _(b=b):
            pf_out[0, b * H : b * H + H] = jnp.zeros((H, H), F32)

    @pl.when(factors)
    def _():
        for q in range(4):
            for b in range(min(q, 1) + 1):

                @pl.when(q != r)
                def _(q=q, b=b):
                    lf_copy(k_here, b, q).start()

                @pl.when(q == r)
                def _(q=q, b=b):
                    lf_out[k_here, b * H : b * H + H] = rleaf[b, q]

    def place_slot(i, carry):
        one = 2 * core - 1
        delta = jnp.where(
            factors,
            jnp.where(i == 0, 0, jnp.where(i == 1, onward, -onward)),
            jnp.where(i == 0, one, -one),
        )
        source = l - delta
        valid = jnp.logical_and(jnp.logical_or(factors, i < 2), inside(source))

        @pl.when(valid)
        def _():
            slot = 2 + delta

            @pl.when(delta != 0)
            def _():
                slot_copy(2, slot, sibling, 0).wait_recv()

            @pl.when(jnp.logical_and(factors, i == 1))
            def _():
                onward_slot().start()

            front = 2 * source + lax.rem(r, 2)
            away = jnp.where(parent_ref[front] == l, 0, 2 * N)
            target = map_ref[pl.ds(front, 1), :] + away
            chosen = (lax.broadcasted_iota(jnp.int32, (N, 256), 0) == target).astype(F32).astype(BF16)
            s = slots[slot]
            square = jnp.concatenate(
                [jnp.concatenate([s[0], s[1]], 1), jnp.concatenate([s[1].T, s[2]], 1)], 0
            )
            high, low = split(square)
            high_rows, low_rows = nn(chosen, high).astype(BF16), nn(chosen, low).astype(BF16)
            for half in range(2):
                rows, columns = slice(256 * half, 256 * half + 256), slice(256 * half, N)
                placed = nt(high_rows[rows], chosen[columns]) + nt(low_rows[rows], chosen[columns])
                for b, (bi, bj) in enumerate(BLOCKS):
                    if bi // 2 == half:
                        ii, jj = (bi - 2 * half) * H, (bj - 2 * half) * H
                        gram[2, b] = gram[2, b] + placed[ii : ii + H, jj : jj + H]

        return carry

    lax.fori_loop(0, 3, place_slot, 0)

    start_first(2)
    for ci in (0, 1, 2):
        next_far(2, ci)
    forward(2, (0, 1, 2), True)

    def pf_copy(b, q):
        return pltpu.make_async_remote_copy(
            src_ref=rpar.at[b, q],
            dst_ref=pf_out.at[0, pl.ds(b * H, H)],
            send_sem=pf_send.at[b, q],
            recv_sem=pf_recv.at[b],
            device_id={"row": q},
            device_id_type=MESH,
        )

    @pl.when(place[2] == 0)
    def _():
        def after(b):
            for q in range(b, 4):

                @pl.when(q != r)
                def _(q=q):
                    pf_copy(b, q).start()

                @pl.when(q == r)
                def _(q=q):
                    pf_out[0, b * H : b * H + H] = rpar[b, q]

        factor(2, 4, rpar, lambda b: None, after)
        for q in range(4):

            @pl.when(q != r)
            def _(q=q):
                for b in range(q + 1):
                    pf_copy(b, q).wait_send()

    @pl.when(place[2] != 0)
    def _():
        for b in range(4):

            @pl.when(b <= r)
            def _(b=b):
                pf_copy(b, 0).wait_recv()

    for k in range(2):

        @pl.when(k_mine != k)
        def _(k=k):
            lf_copy(k, 0, 0).wait_recv()

            @pl.when(r > 0)
            def _():
                lf_copy(k, 1, 0).wait_recv()

        @pl.when(k_mine == k)
        def _(k=k):
            for q in range(4):

                @pl.when(q != r)
                def _(q=q):
                    for b in range(min(q, 1) + 1):
                        lf_copy(k, b, q).wait_send()

    @pl.when(factors)
    def _():
        for delta in (-2, 2):

            @pl.when(inside(l + delta))
            def _(delta=delta):
                own_slot(delta).wait_send()

        sibling_slot().wait_send()

        @pl.when(inside(l - onward))
        def _():
            onward_slot().wait_send()

    for u in range(3):
        drain(u)


def hand_over(leaf_in, parent_in, leaf_out, parent_out, leaf_held, parent_held, sems):
    parts = [
        (leaf_in, leaf_held, leaf_out, (k, pl.ds(h * H, H))) for k in range(2) for h in range(2)
    ] + [(parent_in, parent_held, parent_out, (0, pl.ds(h * H, H))) for h in range(4)]
    inward = [
        pltpu.make_async_copy(source.at[part], held.at[part], sems.at[0, i])
        for i, (source, held, target, part) in enumerate(parts)
    ]
    outward = [
        pltpu.make_async_copy(held.at[part], target.at[part], sems.at[1, i])
        for i, (source, held, target, part) in enumerate(parts)
    ]
    for copy in inward:
        copy.start()
    for arrived, copy in zip(inward, outward):
        arrived.wait()
        copy.start()
    for copy in outward:
        copy.wait()


def per_device(leaf_fronts, front_rows, parent_of, column_map, parent_rows):
    kids, live_rows, _ = leaf_fronts.shape
    chunks = len(CHUNKS)
    dma = pltpu.SemaphoreType.DMA
    vmem = pltpu.VMEM
    factors = pl.pallas_call(
        kernel,
        out_shape=(
            jax.ShapeDtypeStruct((kids, 256, H), F32),
            jax.ShapeDtypeStruct((1, N, H), F32),
        ),
        in_specs=[pl.BlockSpec(memory_space=pltpu.HBM)] * 5,
        out_specs=(pl.BlockSpec(memory_space=pltpu.VMEM),) * 2,
        scratch_shapes=[
            pltpu.SMEM(front_rows.shape, jnp.int32),
            pltpu.SMEM(parent_of.shape, jnp.int32),
            vmem(column_map.shape, jnp.int32),
            vmem((kids, live_rows, N), F32),
            vmem(parent_rows.shape[1:], F32),
            vmem((N, N), F32),
            vmem((N, N), F32),
            vmem((3, 10, H, H), F32),
            vmem((3, 10, H // 2, H), F32),
            vmem((3, 2, 10, H, H), F32),
            vmem((3, H, H), F32),
            vmem((4, H, N), F32),
            vmem((H, H), F32),
            vmem((2, 4, H, H), F32),
            vmem((4, 4, H, H), F32),
            vmem((5, 3, H, H), F32),
            dma((2, 2)),
            dma((4,)),
            dma((3,)),
            dma((3,)),
            dma((3, 2, chunks)),
            dma((3, chunks)),
            dma((3, chunks + 1)),
            dma((3, 2, chunks + 1)),
            dma((2, 4)),
            dma((2, 2)),
            dma((5,)),
            dma((5,)),
            dma((4, 4)),
            dma((4,)),
        ],
        compiler_params=pltpu.CompilerParams(
            collective_id=0, has_side_effects=True, vmem_limit_bytes=60 << 20
        ),
        name="fronts",
    )(front_rows, parent_of, column_map, leaf_fronts, parent_rows)
    hbm = pl.BlockSpec(memory_space=pltpu.HBM)
    return pl.pallas_call(
        hand_over,
        out_shape=[jax.ShapeDtypeStruct(x.shape, x.dtype) for x in factors],
        in_specs=[hbm] * 2,
        out_specs=[hbm] * 2,
        scratch_shapes=[vmem(x.shape, x.dtype) for x in factors] + [dma((2, 8))],
        name="hand_over",
    )(*factors)


def solution(mesh):
    return jax.shard_map(
        per_device,
        mesh=mesh,
        in_specs=(P("leaf", "row", None), P("leaf"), P(), P(), P("leaf", "row", None)),
        out_specs=(P("leaf", None, "row"), P("leaf", None, "row")),
        check_vma=False,
    )
```
